256 devices in a mesh: depth: 32 (over z, y), height: 8 (over x, core).
Axes of the slice: x: 4, y: 4, z: 8, core: 2. Of those that a mesh axis runs over, the one named last changes fastest.
Arguments:
- features: bfloat16 [32, 384, 256, 128], P(None, 'depth', 'height'), may hold values from -6 to 6
- head_weight: bfloat16 [3, 32], replicated, may hold values from -1 to 1
- head_bias: float32 [3], replicated, may hold values from -3 to 3
- labels: int32 [3, 384, 256, 128], P(None, 'depth', 'height'), may hold values from 0 to 1
- label_skeleton: int32 [3, 384, 256, 128], P(None, 'depth', 'height'), may hold values from 0 to 1
Outputs:
- loss: float32 [], replicated
- grad_features: bfloat16 [32, 384, 256, 128], P(None, 'depth', 'height')
- head_update: float32 [3, 32], replicated
- bias_update: float32 [3], replicated
The draws below stay inside these ranges and needn't reach their ends.
All inputs are finite; a program needn't handle non-finite values.
Results may differ from the reference program's by a relative error of at most 0.0016.
Values sent between devices are 32-bit elements; how exact they have to be, the bound alone decides.
No kernel may reach another device: no remote copies, remote signals or barrier semaphores. Data moves between devices by JAX's collectives and lax.ppermute only.
A program may use at most 128 MiB of HBM per device.

```python
import jax
import jax.numpy as jnp
from jax import lax

C = 32
K = 3
WD = 128
ITERS = 3
ND = 384
NH = 256
TOTAL_CELLS = 12582912


def draw_labels(key, part):
    key = jax.random.fold_in(key, 11)
    depth_idx = lax.broadcasted_iota(jnp.int32, (K, ND, NH, WD), 1)
    thresh = 150 + 450 * depth_idx // ND
    ticket = jax.random.randint(key, (K, ND, NH, WD), 0, 1000)
    return (ticket < thresh).astype(jnp.int32)


def draw_label_skeleton(key, part):
    key = jax.random.fold_in(key, 23)
    depth_idx = lax.broadcasted_iota(jnp.int32, (K, ND, NH, WD), 1)
    thresh = 40 + 160 * depth_idx // ND
    ticket = jax.random.randint(key, (K, ND, NH, WD), 0, 1000)
    return (ticket < thresh).astype(jnp.int32)


def block_scale(key, shape, cuts, least, top_value):
    gain, own = 1.0, jax.random.fold_in(key, 6)
    for axis_at, parts in cuts:
        draws = jnp.exp(jax.random.uniform(jax.random.fold_in(own, axis_at), (parts,), jnp.float32, least / len(cuts), top_value / len(cuts)))
        gain = gain * jnp.repeat(draws, shape[axis_at] // parts).reshape([-1 if axis == axis_at else 1 for axis in range(len(shape))])
    return gain


def bell_draw(own_key, extent, deviation, reach, pieces=(), dtype=jnp.bfloat16):
    factor_of = block_scale(own_key, extent, pieces, -0.22, 0.18) if pieces else 1.0
    array = jax.random.normal(own_key, extent, jnp.float32) * deviation * factor_of
    return jnp.minimum(jnp.maximum(array, -reach), reach).astype(dtype)


def setup_inputs(seed: int = 0) -> dict:
    keys = jax.random.split(jax.random.key(seed), 6)
    features = bell_draw(keys[0], (C, ND, NH, WD), 1.0, 6.0, ((1, 32), (2, 8)))
    head_weight = bell_draw(keys[1], (K, C), C ** -0.5, 1.0)
    head_bias = bell_draw(keys[2], (K,), 1.0, 3.0, (), jnp.float32)
    labels = draw_labels(jax.random.fold_in(keys[5], 71), 0)
    label_skeleton = draw_label_skeleton(jax.random.fold_in(keys[5], 71), 0)
    return {"features": features, "head_weight": head_weight, "head_bias": head_bias, "labels": labels, "label_skeleton": label_skeleton}


TAU = 0.1
SHARP = 0.05
ALPHA = 0.3
BETA = 0.7

def box_sum(v):
    lead = ((0, 0),) * (v.ndim - 3)
    padded = jnp.pad(v, lead + ((1, 1), (1, 1), (1, 1)))
    total = padded[..., :-2, :, :] + padded[..., 1:-1, :, :] + padded[..., 2:, :, :]
    total = total[..., :, :-2, :] + total[..., :, 1:-1, :] + total[..., :, 2:, :]
    return total[..., :-2] + total[..., 1:-1] + total[..., 2:]

def pooled(x, sign):
    return sign * TAU * jnp.log(box_sum(jnp.exp(sign * x / TAU)))

def smooth(v):
    return SHARP * jax.nn.softplus(v / SHARP)

def skeleton(prob):
    eroded = pooled(prob, -1.0)
    skel = smooth(prob - pooled(eroded, 1.0))
    current = eroded
    for step in range(ITERS):
        eroded = pooled(current, -1.0)
        delta = smooth(current - pooled(eroded, 1.0))
        skel = skel + smooth(delta - skel * delta)
        current = eroded
    return skel

def class_term(tp, sp, sl, sky, sk, lsp, ls):
    prec = (sky + 1.0) / (sk + 1.0)
    sens = (lsp + 1.0) / (ls + 1.0)
    cldice = 1.0 - 2.0 * prec * sens / (prec + sens)
    tversky = (tp + 1.0) / (tp + ALPHA * (sp - tp) + BETA * (sl - tp) + 1.0)
    return cldice + 1.0 - tversky

def reference(features, head_weight, head_bias, labels, label_skeleton):

    def one_class(inputs):
        w_row, bias, lab, lsk = inputs

        def accumulate(acc, pair):
            w_one, f_one = pair
            return (acc + w_one.astype(jnp.float32) * f_one.astype(jnp.float32), None)
        start = jnp.zeros((ND, NH, WD), jnp.float32)
        logits, unused = lax.scan(accumulate, start, (w_row, features))
        logits = logits + bias.astype(jnp.float32)
        labf = lab.astype(jnp.float32)
        lskf = lsk.astype(jnp.float32)

        def objective(lg):
            prob = jax.nn.sigmoid(lg)
            skel = skeleton(prob)
            return class_term(jnp.sum(prob * labf), jnp.sum(prob), jnp.sum(labf), jnp.sum(skel * labf), jnp.sum(skel), jnp.sum(lskf * prob), jnp.sum(lskf))
        term, pull = jax.vjp(objective, logits)
        dlg, = pull(jnp.ones_like(term) * (TOTAL_CELLS / K))
        return (term, dlg)
    terms, dlogit = lax.map(one_class, (head_weight, head_bias, labels, label_skeleton))
    loss = jnp.mean(terms)
    weight_cols = head_weight.astype(jnp.float32).T

    def feature_grad(w_col):
        return jnp.tensordot(w_col, dlogit, axes=1, precision=lax.Precision.HIGHEST).astype(jnp.bfloat16)
    grad_features = lax.map(feature_grad, weight_cols)
    dlow = lax.optimization_barrier(dlogit.astype(jnp.bfloat16)).astype(jnp.float32)

    def weight_grad(f_one):
        return lax.optimization_barrier(jnp.sum(dlow * f_one.astype(jnp.float32)[None], axis=(1, 2, 3)))
    grad_w = lax.map(weight_grad, features).T
    grad_b = lax.optimization_barrier(jnp.sum(dlogit, axis=(1, 2, 3)))
    rms = jnp.sqrt((jnp.sum(grad_w * grad_w) + jnp.sum(grad_b * grad_b)) / (K * C + K) + 1e-06)
    return (loss, grad_features, grad_w / rms, grad_b / rms)
```

```python
import jax
import jax.numpy as jnp
from jax import lax
from jax.experimental import pallas as pl
from jax.experimental.pallas import tpu as pltpu
from jax.sharding import PartitionSpec as P

ITERS = 3
TAU = 0.1
SHARP = 0.05
ALPHA = 0.3
BETA = 0.7
HALO = 10
LHALO = 5
ROWS = 80
OFF = 24
NB = 4


def class_term(totals):
    tp, sp, sl, sky, sk, lsp, ls = [totals[i] for i in range(7)]
    prec = (sky + 1.0) / (sk + 1.0)
    sens = (lsp + 1.0) / (ls + 1.0)
    cldice = 1.0 - 2.0 * prec * sens / (prec + sens)
    tversky = (tp + 1.0) / (tp + ALPHA * (sp - tp) + BETA * (sl - tp) + 1.0)
    return cldice + 1.0 - tversky


def shift(value, axis, step):
    n = lax.axis_size(axis)
    pairs = [(i, i + step) for i in range(n) if 0 <= i + step < n]
    return lax.ppermute(value, axis, pairs)


def exchange(value, dim, width, axis):
    n = value.shape[dim]
    before = shift(lax.slice_in_dim(value, n - width, n, axis=dim), axis, 1)
    after = shift(lax.slice_in_dim(value, 0, width, axis=dim), axis, -1)
    return before, after


def wide_sum(s, lane):
    width = s.shape[-1]
    left = jnp.where(lane == 0, 0.0, pltpu.roll(s, 1, 1))
    right = jnp.where(lane == width - 1, 0.0, pltpu.roll(s, width - 1, 1))
    return s + left + right


def boxes(load, d, r0, nr, lane):
    h = []
    for i in range(NB + 2):
        h.append(load(d + i - 1, r0 - 1, nr) + load(d + i - 1, r0, nr) + load(d + i - 1, r0 + 1, nr))
    out = []
    for i in range(0, NB, 2):
        mid = h[i + 1] + h[i + 2]
        out.append(wide_sum(h[i] + mid, lane))
        out.append(wide_sum(mid + h[i + 3], lane))
    return out


def sweep(first, last, body):
    count = -(-(last - first) // NB)

    def step(i, carry):
        body(jnp.minimum(first + i * NB, last - NB))
        return carry

    lax.fori_loop(0, count, step, 0)


def core(
    e_own, e_dlo, e_dhi, e_hlo, e_hhi, l_own, l_dlo, l_dhi, l_hlo, l_hhi, p_own, k_own,
    ga_ref, gb_ref, part_ref,
    E, R, X, U, V, Q, L,
):
    depth, height = p_own.shape[1], p_own.shape[2]
    planes = depth + 2 * HALO
    wd = p_own.shape[3]
    lane8 = lax.broadcasted_iota(jnp.int32, (8, wd), 1)
    base = HALO - LHALO
    E[0, :, OFF - HALO - 8 : OFF, :] = jnp.zeros((planes, HALO + 8, wd), jnp.float32)
    E[0, :, OFF + height : OFF + height + HALO + 8, :] = jnp.zeros((planes, HALO + 8, wd), jnp.float32)
    E[0, HALO : HALO + depth, OFF : OFF + height, :] = e_own[0]
    E[0, 0:HALO, OFF : OFF + height, :] = e_dlo[0]
    E[0, HALO + depth :, OFF : OFF + height, :] = e_dhi[0]
    E[0, :, OFF - HALO : OFF, :] = e_hlo[0]
    E[0, :, OFF + height : OFF + height + HALO, :] = e_hhi[0]
    lplanes = depth + 2 * LHALO
    L[:, OFF - 8 : OFF, :] = jnp.zeros((lplanes, 8, wd), jnp.float32)
    L[:, OFF + height : OFF + height + 8, :] = jnp.zeros((lplanes, 8, wd), jnp.float32)
    L[LHALO : LHALO + depth, OFF : OFF + height, :] = l_own[0]
    L[0:LHALO, OFF : OFF + height, :] = l_dlo[0]
    L[LHALO + depth :, OFF : OFF + height, :] = l_dhi[0]
    L[:, OFF - LHALO : OFF, :] = l_hlo[0]
    L[:, OFF + height : OFF + height + LHALO, :] = l_hhi[0]

    w0, wn = OFF - 8, height + 16
    lane = lax.broadcasted_iota(jnp.int32, (wn, wd), 1)
    lane_big = lax.broadcasted_iota(jnp.int32, (wn + 16, wd), 1)

    for j in range(ITERS + 1):
        r0, nr, ln = (w0 - 8, wn + 16, lane_big) if j == 0 else (w0, wn, lane)

        def erode(d, j=j, r0=r0, nr=nr, ln=ln):
            outs = boxes(lambda a, b, n: E[j, a, pl.ds(b, n), :], d, r0, nr, ln)
            for i, s in enumerate(outs):
                live = E[0, d + i, pl.ds(r0, nr), :] > 0.0
                E[j + 1, d + i, pl.ds(r0, nr), :] = jnp.where(live, s, 0.0)
                R[j, d + i, pl.ds(r0, nr), :] = jnp.where(live, 1.0 / s, 0.0)

        sweep(j + 1, planes - j - 1, erode)

    for j in range(ITERS + 1):

        def dilate(d, j=j):
            outs = boxes(lambda a, b, n: R[j, a, pl.ds(b, n), :], d, w0, wn, lane)
            for i, s in enumerate(outs):
                live = E[0, d + i, pl.ds(w0, wn), :] > 0.0
                rd = 1.0 / s
                t = rd / E[j, d + i, pl.ds(w0, wn), :]
                U[j, d + i - base, pl.ds(w0, wn), :] = jnp.where(live, rd, 0.0)
                X[j, d + i - base, pl.ds(w0, wn), :] = jnp.where(live, t * t, 0.0)

        sweep(base, planes - base, dilate)

    def point(i, carry):
        d = i // (wn // 8)
        r = pl.multiple_of(w0 + 8 * (i % (wn // 8)), 8)
        x = [X[j, d, pl.ds(r, 8), :] for j in range(ITERS + 1)]
        opx = [1.0 + v for v in x]
        delta = [SHARP * jnp.log(v) for v in opx]
        skel = delta[0]
        om, su = [None], [None]
        for j in range(1, ITERS + 1):
            om.append(1.0 - skel)
            e = jnp.exp(delta[j] * om[j] * (1.0 / SHARP))
            ope = 1.0 + e
            skel = skel + SHARP * jnp.log(ope)
            su.append(e / ope)
        lab = L[d, pl.ds(r, 8), :]
        g = None
        for j in range(ITERS, 0, -1):
            sj = su[j] if g is None else su[j] * g
            gv = sj * om[j] * (x[j] / opx[j])
            keep = 1.0 - su[j] * delta[j]
            g = keep if g is None else g * keep
            u = gv * U[j, d, pl.ds(r, 8), :]
            X[j, d, pl.ds(r, 8), :] = gv
            U[j, d, pl.ds(r, 8), :] = u
            V[j, d, pl.ds(r, 8), :] = u * lab
        gv = g * (x[0] / opx[0])
        u = gv * U[0, d, pl.ds(r, 8), :]
        X[0, d, pl.ds(r, 8), :] = gv
        U[0, d, pl.ds(r, 8), :] = u
        V[0, d, pl.ds(r, 8), :] = u * lab
        own = (d >= LHALO) & (d < LHALO + depth) & (r >= OFF) & (r < OFF + height)
        f = jnp.where(own, 1.0, 0.0)
        skel = skel * f
        return carry[0] + skel * lab, carry[1] + skel

    zero = jnp.zeros((8, wd), jnp.float32)
    sky, sk = lax.fori_loop(0, lplanes * (wn // 8), point, (zero, zero))
    part_ref[0, 3] = sky
    part_ref[0, 4] = sk

    for j in range(ITERS + 1, 0, -1):
        now, nxt = j % 2, (j + 1) % 2

        def back(d, j=j, now=now, nxt=nxt):
            b = d - base
            for side, src in ((0, V), (1, U)):
                du = boxes(lambda a, c, n: src[j - 1, a, pl.ds(c, n), :], b, w0, wn, lane)
                if j <= ITERS:
                    dq = boxes(lambda a, c, n: Q[side, nxt, a, pl.ds(c, n), :], b, w0, wn, lane)
                for i in range(NB):
                    live = E[0, d + i, pl.ds(w0, wn), :] > 0.0
                    r = R[j - 1, d + i, pl.ds(w0, wn), :]
                    v = -r * du[i]
                    if j <= ITERS:
                        gv = X[j, b + i, pl.ds(w0, wn), :]
                        if side == 0:
                            gv = gv * L[b + i, pl.ds(w0, wn), :]
                        v = r * (gv + v) + dq[i]
                        v = jnp.where(live, v, 0.0)
                    else:
                        v = r * v
                    Q[side, now, b + i, pl.ds(w0, wn), :] = v

        first = HALO - j
        sweep(first, planes - first, back)

    lane_own = lax.broadcasted_iota(jnp.int32, (height, wd), 1)

    def last(d):
        b = d - base
        o = d - HALO
        for side, out in ((0, ga_ref), (1, gb_ref)):
            dq = boxes(lambda a, c, n: Q[side, 1, a, pl.ds(c, n), :], b, OFF, height, lane_own)
            for i in range(NB):
                gv = X[0, b + i, pl.ds(OFF, height), :]
                if side == 0:
                    gv = gv * L[b + i, pl.ds(OFF, height), :]
                out[0, o + i] = gv + E[0, d + i, pl.ds(OFF, height), :] * dq[i]

    sweep(HALO, HALO + depth, last)

    def sums(o, carry):
        tp, sp, sl, lsp, ls = carry
        for t in range(height // 8):
            p = p_own[0, o, pl.ds(8 * t, 8), :]
            y = l_own[0, o, pl.ds(8 * t, 8), :]
            k = k_own[0, o, pl.ds(8 * t, 8), :].astype(jnp.float32)
            tp, sp, sl, lsp, ls = tp + p * y, sp + p, sl + y, lsp + k * p, ls + k
        return tp, sp, sl, lsp, ls

    tp, sp, sl, lsp, ls = lax.fori_loop(0, depth, sums, (zero,) * 5)
    part_ref[0, 0] = tp
    part_ref[0, 1] = sp
    part_ref[0, 2] = sl
    part_ref[0, 5] = lsp
    part_ref[0, 6] = ls


def run_core(own, dlo, dhi, hlo, hhi, lab, ldlo, ldhi, lhlo, lhhi, prob, lsk):
    classes, depth, height, wd = prob.shape
    planes = depth + 2 * HALO
    lplanes = depth + 2 * LHALO
    args = (own, dlo, dhi, hlo, hhi, lab, ldlo, ldhi, lhlo, lhhi, prob, lsk)

    def spec(v):
        return pl.BlockSpec((1,) + v.shape[1:], lambda k: (k,) + (0,) * (len(v.shape) - 1))

    full = jax.ShapeDtypeStruct(prob.shape, jnp.float32)
    part = jax.ShapeDtypeStruct((classes, 7, 8, wd), jnp.float32)
    n = ITERS + 1
    return pl.pallas_call(
        core,
        grid=(classes,),
        in_specs=[spec(v) for v in args],
        out_specs=[spec(full), spec(full), spec(part)],
        out_shape=[full, full, part],
        scratch_shapes=[
            pltpu.VMEM((n + 1, planes, ROWS, wd), jnp.float32),
            pltpu.VMEM((n, planes, ROWS, wd), jnp.float32),
            pltpu.VMEM((n, lplanes, ROWS, wd), jnp.float32),
            pltpu.VMEM((n, lplanes, ROWS, wd), jnp.float32),
            pltpu.VMEM((n, lplanes, ROWS, wd), jnp.float32),
            pltpu.VMEM((2, 2, lplanes, ROWS, wd), jnp.float32),
            pltpu.VMEM((lplanes, ROWS, wd), jnp.float32),
        ],
        compiler_params=pltpu.CompilerParams(vmem_limit_bytes=56 * 2**20),
        name="skeleton",
    )(*args)


def all_sum(value):
    for axis in ("height", "depth"):
        n = lax.axis_size(axis)
        spread = jnp.broadcast_to(value[None], (n,) + value.shape)
        value = jnp.sum(lax.all_to_all(spread, axis, 0, 0, tiled=True), axis=0)
    return value


def per_device(features, head_weight, head_bias, labels, label_skeleton):
    classes, channels = head_weight.shape
    _, block_d, block_h, wd = features.shape
    total_cells = block_d * lax.axis_size("depth") * block_h * lax.axis_size("height") * wd
    labf = labels.astype(jnp.float32)
    ldlo, ldhi = exchange(labf, 1, LHALO, "depth")
    ltall = jnp.concatenate([ldlo, labf, ldhi], axis=1)
    lhlo, lhhi = exchange(ltall, 2, LHALO, "height")
    logits = jnp.einsum("kc,cdhw->kdhw", head_weight, features, preferred_element_type=jnp.float32)
    logits = logits + head_bias[:, None, None, None]
    prob = jax.nn.sigmoid(logits)
    own = jnp.exp(-prob / TAU)
    dlo, dhi = exchange(own, 1, HALO, "depth")
    tall = jnp.concatenate([dlo, own, dhi], axis=1)
    hlo, hhi = exchange(tall, 2, HALO, "height")
    ga, gb, part = run_core(
        own, dlo, dhi, hlo, hhi, labf, ldlo, ldhi, lhlo, lhhi, prob, label_skeleton
    )
    lskf = label_skeleton.astype(jnp.float32)
    slope = prob * (1.0 - prob)
    fields = jnp.stack([slope * labf, slope, slope * ga, slope * gb, slope * lskf], axis=1)
    high = fields.astype(jnp.bfloat16)
    low = lax.optimization_barrier((fields - high.astype(jnp.float32)).astype(jnp.bfloat16))
    heads = jnp.einsum("kfdhw,cdhw->kfc", high, features, preferred_element_type=jnp.float32)
    heads = heads + jnp.einsum("kfdhw,cdhw->kfc", low, features, preferred_element_type=jnp.float32)
    local = jnp.concatenate(
        [
            heads.reshape(-1),
            jnp.sum(fields, axis=(2, 3, 4)).reshape(-1),
            jnp.sum(part, axis=(2, 3)).reshape(-1),
            jnp.zeros((-classes * (5 * (channels + 1) + 7) % 1024,), jnp.float32),
        ]
    ).reshape(-1, 128)
    whole = all_sum(local).reshape(-1)
    cut = classes * 5 * channels
    heads = whole[:cut].reshape(classes, 5, channels)
    biases = whole[cut : cut + classes * 5].reshape(classes, 5)
    totals = whole[cut + classes * 5 : cut + classes * 12].reshape(classes, 7).T
    loss = jnp.sum(class_term(totals)) / classes
    scale = total_cells / classes
    dtot = jax.grad(lambda t: jnp.sum(class_term(t)))(totals) * scale
    coef = jnp.stack([dtot[0], dtot[1], dtot[3], dtot[4], dtot[5]])
    grad_w = jnp.sum(coef.T[:, :, None] * heads, axis=1)
    grad_b = jnp.sum(coef.T * biases, axis=1)
    c = coef[:, :, None, None, None]
    dlogit = slope * (c[0] * labf + c[1] + c[2] * ga + c[3] * gb + c[4] * lskf)
    grad_features = sum(
        head_weight[k].astype(jnp.float32)[:, None, None, None] * dlogit[k][None] for k in range(classes)
    ).astype(jnp.bfloat16)
    rms = jnp.sqrt(
        (jnp.sum(grad_w * grad_w) + jnp.sum(grad_b * grad_b)) / (classes * channels + classes)
        + 1e-06
    )
    return (loss, grad_features, grad_w / rms, grad_b / rms)


def solution(mesh):
    return jax.shard_map(
        per_device,
        mesh=mesh,
        in_specs=(
            P(None, "depth", "height", None),
            P(),
            P(),
            P(None, "depth", "height", None),
            P(None, "depth", "height", None),
        ),
        out_specs=(P(), P(None, "depth", "height", None), P(), P()),
        check_vma=False,
    )
```

```python
import functools

import jax
import jax.numpy as jnp
from jax import lax
from jax.experimental import pallas as pl
from jax.experimental.pallas import tpu as pltpu
from jax.sharding import PartitionSpec as P

ITERS = 3
TAU = 0.1
SHARP = 0.05
ALPHA = 0.3
BETA = 0.7
HALO = 10
LHALO = 5
ROWS = 80
OFF = 24
NB = 4
MXU = 2
FIELDS = 5
EXACT = lax.Precision.HIGHEST
LAST = (((1,), (1,)), ((), ()))


def shift(value, axis, step):
    n = lax.axis_size(axis)
    pairs = [(i, i + step) for i in range(n) if 0 <= i + step < n]
    return lax.ppermute(value, axis, pairs)


def head_kernel(w_ref, b_ref, f_ref, l_ref, p_ref, e_ref, first_ref, last_ref):
    d = pl.program_id(0)
    depth = pl.num_programs(0)
    channels = f_ref.shape[0]
    height = f_ref.shape[2]
    classes = p_ref.shape[0]
    acc = [None] * classes
    for c in range(channels):
        f = f_ref[c, 0].astype(jnp.float32)
        for k in range(classes):
            term = w_ref[k, c] * f
            acc[k] = term if c == 0 else acc[k] + term
    exps, labs = [], []
    for k in range(classes):
        prob = 1.0 / (1.0 + jnp.exp(-(acc[k] + b_ref[k])))
        p_ref[k, 0] = prob
        exps.append(jnp.exp(prob * (-1.0 / TAU)))
        e_ref[k, 0] = exps[k]
        labs.append(l_ref[k, 0].astype(jnp.float32))

    def put(ref, row, values):
        for k in range(classes):
            ref[k, pl.ds(pl.multiple_of(row * height, height), height), :] = values[k]

    @pl.when(d < HALO)
    def _():
        put(first_ref, d, exps)

    @pl.when(d >= depth - HALO)
    def _():
        put(last_ref, d - (depth - HALO), exps)

    @pl.when(d < LHALO)
    def _():
        put(first_ref, HALO + d, labs)

    @pl.when(d >= depth - LHALO)
    def _():
        put(last_ref, HALO + d - (depth - LHALO), labs)


def run_head(weight, bias, features, labels):
    classes, depth, height, wd = labels.shape
    channels = features.shape[0]
    plane = pl.BlockSpec((classes, 1, height, wd), lambda d: (0, d, 0, 0))
    rows = (HALO + LHALO) * height
    strip = pl.BlockSpec((classes, rows, wd), lambda d: (0, 0, 0))
    full = jax.ShapeDtypeStruct(labels.shape, jnp.float32)
    edge = jax.ShapeDtypeStruct((classes, rows, wd), jnp.float32)
    return pl.pallas_call(
        head_kernel,
        grid=(depth,),
        in_specs=[
            pl.BlockSpec(memory_space=pltpu.SMEM),
            pl.BlockSpec(memory_space=pltpu.SMEM),
            pl.BlockSpec((channels, 1, height, wd), lambda d: (0, d, 0, 0)),
            plane,
        ],
        out_specs=[plane, plane, strip, strip],
        out_shape=[full, full, edge, edge],
        compiler_params=pltpu.CompilerParams(vmem_limit_bytes=32 * 2**20),
        name="head",
    )(weight, bias, features, labels)


def side_kernel(e_ref, l_ref, lo_ref, hi_ref, first_ref, last_ref):
    depth, height = e_ref.shape[1], e_ref.shape[2]
    for out, near in ((first_ref, True), (last_ref, False)):
        for p in range(depth + 2 * HALO):
            at = 0 if near else height - HALO
            if p < HALO:
                v = lo_ref[0, pl.ds(p * height + at, HALO), :]
            elif p < HALO + depth:
                v = e_ref[0, p - HALO, pl.ds(at, HALO), :]
            else:
                v = hi_ref[0, pl.ds((p - HALO - depth) * height + at, HALO), :]
            out[0, pl.ds(p * HALO, HALO), :] = v
        base = HALO * (depth + 2 * HALO)
        for p in range(depth + 2 * LHALO):
            at = 0 if near else height - LHALO
            if p < LHALO:
                v = lo_ref[0, pl.ds((HALO + p) * height + at, LHALO), :]
            elif p < LHALO + depth:
                v = l_ref[0, p - LHALO, pl.ds(at, LHALO), :].astype(jnp.float32)
            else:
                v = hi_ref[0, pl.ds((HALO + p - LHALO - depth) * height + at, LHALO), :]
            out[0, pl.ds(base + p * LHALO, LHALO), :] = v


def by_class(v):
    return pl.BlockSpec((1,) + v.shape[1:], lambda k: (k,) + (0,) * (len(v.shape) - 1))


def run_side(own, labels, lo, hi):
    classes, depth, height, wd = own.shape
    rows = HALO * (depth + 2 * HALO) + LHALO * (depth + 2 * LHALO)
    edge = jax.ShapeDtypeStruct((classes, rows, wd), jnp.float32)
    args = (own, labels, lo, hi)
    return pl.pallas_call(
        side_kernel,
        grid=(classes,),
        in_specs=[by_class(v) for v in args],
        out_specs=[by_class(edge)] * 2,
        out_shape=[edge, edge],
        compiler_params=pltpu.CompilerParams(vmem_limit_bytes=32 * 2**20),
        name="side",
    )(*args)


def wide_sums(values, lane, band):
    rows, width = values[0].shape
    out = []
    if MXU:
        s = jnp.concatenate(values[:MXU], axis=0)
        high = s.astype(jnp.bfloat16)
        low = (s - high.astype(jnp.float32)).astype(jnp.bfloat16)
        s = jnp.dot(jnp.concatenate([high, low], axis=1), band, preferred_element_type=jnp.float32)
        out = [s[i * rows : (i + 1) * rows] for i in range(MXU)]
    for s in values[MXU:]:
        left = jnp.where(lane == 0, 0.0, pltpu.roll(s, 1, 1))
        right = jnp.where(lane == width - 1, 0.0, pltpu.roll(s, width - 1, 1))
        out.append(s + left + right)
    return out


def boxes(load, d, r0, nr, lane, band):
    h = []
    for i in range(NB + 2):
        h.append(load(d + i - 1, r0 - 1, nr) + load(d + i - 1, r0, nr) + load(d + i - 1, r0 + 1, nr))
    out = []
    for i in range(0, NB, 2):
        mid = h[i + 1] + h[i + 2]
        out.append(h[i] + mid)
        out.append(mid + h[i + 3])
    return wide_sums(out, lane, band)


def sweep(first, last, body):
    for i in range(first, last, NB):
        body(min(i, last - NB))


def core_kernel(
    f_ref, e_own, e_lo, e_hi, e_left, e_right, l_own, p_own, k_own,
    x_ref, sum_ref,
    E, R, X, U, V, Q, L, S, A, T, B,
):
    k = pl.program_id(0)
    depth, height, wd = p_own.shape[1:]
    planes = depth + 2 * HALO
    lplanes = depth + 2 * LHALO
    base = HALO - LHALO
    side = HALO * planes

    @pl.when(k == 0)
    def _():
        row = lax.broadcasted_iota(jnp.int32, (2 * wd, wd), 0)
        col = lax.broadcasted_iota(jnp.int32, (2 * wd, wd), 1)
        near = jnp.abs(jnp.where(row < wd, row, row - wd) - col) <= 1
        B[...] = jnp.where(near, 1.0, 0.0).astype(jnp.bfloat16)

    E[0, :, OFF - HALO - 8 : OFF - HALO, :] = jnp.zeros((planes, 8, wd), jnp.float32)
    E[0, :, OFF + height + HALO : OFF + height + HALO + 8, :] = jnp.zeros((planes, 8, wd), jnp.float32)
    E[0, HALO : HALO + depth, OFF : OFF + height, :] = e_own[0]
    for p in range(HALO):
        E[0, p, OFF : OFF + height, :] = e_lo[0, p * height : (p + 1) * height, :]
        E[0, HALO + depth + p, OFF : OFF + height, :] = e_hi[0, p * height : (p + 1) * height, :]
    for p in range(planes):
        E[0, p, OFF - HALO : OFF, :] = e_left[0, p * HALO : (p + 1) * HALO, :]
        E[0, p, OFF + height : OFF + height + HALO, :] = e_right[0, p * HALO : (p + 1) * HALO, :]
    L[:, OFF - 8 : OFF - LHALO, :] = jnp.zeros((lplanes, 8 - LHALO, wd), jnp.float32)
    L[:, OFF + height + LHALO : OFF + height + 8, :] = jnp.zeros((lplanes, 8 - LHALO, wd), jnp.float32)
    L[LHALO : LHALO + depth, OFF : OFF + height, :] = l_own[0].astype(jnp.float32)
    for p in range(LHALO):
        at = (HALO + p) * height
        L[p, OFF : OFF + height, :] = e_lo[0, at : at + height, :]
        L[LHALO + depth + p, OFF : OFF + height, :] = e_hi[0, at : at + height, :]
    for p in range(lplanes):
        at = side + p * LHALO
        L[p, OFF - LHALO : OFF, :] = e_left[0, at : at + LHALO, :]
        L[p, OFF + height : OFF + height + LHALO, :] = e_right[0, at : at + LHALO, :]

    band = B[...]
    w0, wn = OFF - 8, height + 16
    lane = lax.broadcasted_iota(jnp.int32, (wn, wd), 1)
    lane_big = lax.broadcasted_iota(jnp.int32, (wn + 16, wd), 1)
    lane_own = lax.broadcasted_iota(jnp.int32, (height, wd), 1)

    for j in range(ITERS + 1):
        r0, nr, ln = (w0 - 8, wn + 16, lane_big) if j == 0 else (w0, wn, lane)

        def erode(d, j=j, r0=r0, nr=nr, ln=ln):
            outs = boxes(lambda a, b, n: E[j, a, pl.ds(b, n), :], d, r0, nr, ln, band)
            for i, s in enumerate(outs):
                live = E[0, d + i, pl.ds(r0, nr), :] > 0.0
                E[j + 1, d + i, pl.ds(r0, nr), :] = jnp.where(live, s, 0.0)
                R[j, d + i, pl.ds(r0, nr), :] = jnp.where(live, 1.0 / s, 0.0)

        sweep(j + 1, planes - j - 1, erode)

    for j in range(ITERS + 1):

        def dilate(d, j=j):
            outs = boxes(lambda a, b, n: R[j, a, pl.ds(b, n), :], d, w0, wn, lane, band)
            for i, s in enumerate(outs):
                live = E[0, d + i, pl.ds(w0, wn), :] > 0.0
                rd = 1.0 / s
                t = rd / E[j, d + i, pl.ds(w0, wn), :]
                U[j, d + i - base, pl.ds(w0, wn), :] = jnp.where(live, rd, 0.0)
                X[j, d + i - base, pl.ds(w0, wn), :] = jnp.where(live, t * t, 0.0)

        sweep(base, planes - base, dilate)

    row = lax.broadcasted_iota(jnp.int32, (wn, wd), 0)
    inner = jnp.where((row >= OFF - w0) & (row < OFF - w0 + height), 1.0, 0.0)

    def point(d, carry):
        rows = pl.ds(w0, wn)
        x = [X[j, d, rows, :] for j in range(ITERS + 1)]
        opx = [1.0 + v for v in x]
        delta = [SHARP * jnp.log(v) for v in opx]
        skel = delta[0]
        om, su = [None], [None]
        for j in range(1, ITERS + 1):
            om.append(1.0 - skel)
            e = jnp.exp(delta[j] * om[j] * (1.0 / SHARP))
            ope = 1.0 + e
            skel = skel + SHARP * jnp.log(ope)
            su.append(e / ope)
        lab = L[d, rows, :]
        g = None
        for j in range(ITERS, -1, -1):
            gv = x[j] / opx[j]
            if j:
                gv = gv * su[j] * om[j]
            if g is not None:
                gv = gv * g
            if j:
                keep = 1.0 - su[j] * delta[j]
                g = keep if g is None else g * keep
            u = gv * U[j, d, rows, :]
            X[j, d, rows, :] = gv
            U[j, d, rows, :] = u
            V[j, d, rows, :] = u * lab
        own = jnp.where((d >= LHALO) & (d < LHALO + depth), 1.0, 0.0)
        skel = skel * (inner * own)
        return carry[0] + skel * lab, carry[1] + skel

    zero = jnp.zeros((wn, wd), jnp.float32)
    sky, sk = lax.fori_loop(0, lplanes, point, (zero, zero), unroll=2)

    for j in range(ITERS + 1, 0, -1):
        now, nxt = j % 2, (j + 1) % 2

        def back(d, j=j, now=now, nxt=nxt):
            b = d - base
            for which, src in ((0, V), (1, U)):
                du = boxes(lambda a, c, n: src[j - 1, a, pl.ds(c, n), :], b, w0, wn, lane, band)
                if j <= ITERS:
                    dq = boxes(lambda a, c, n: Q[which, nxt, a, pl.ds(c, n), :], b, w0, wn, lane, band)
                for i in range(NB):
                    r = R[j - 1, d + i, pl.ds(w0, wn), :]
                    v = -r * du[i]
                    if j <= ITERS:
                        live = E[0, d + i, pl.ds(w0, wn), :] > 0.0
                        gv = X[j, b + i, pl.ds(w0, wn), :]
                        if which == 0:
                            gv = gv * L[b + i, pl.ds(w0, wn), :]
                        v = jnp.where(live, r * (gv + v) + dq[i], 0.0)
                    else:
                        v = r * v
                    Q[which, now, b + i, pl.ds(w0, wn), :] = v

        sweep(HALO - j, planes - HALO + j, back)

    sums = [jnp.zeros((height, wd), jnp.float32) for _ in range(5 + FIELDS)]

    def last(d):
        b = d - base
        o = d - HALO
        grads = [
            boxes(lambda a, c, n: Q[which, 1, a, pl.ds(c, n), :], b, OFF, height, lane_own, band)
            for which in range(2)
        ]
        for i in range(NB):
            e = E[0, d + i, pl.ds(OFF, height), :]
            gv = X[0, b + i, pl.ds(OFF, height), :]
            prob = p_own[0, o + i]
            lab = L[b + i, pl.ds(OFF, height), :]
            lsk = k_own[0, o + i].astype(jnp.float32)
            slope = prob * (1.0 - prob)
            fields = [
                slope * lab,
                slope,
                slope * (gv * lab + e * grads[0][i]),
                slope * (gv + e * grads[1][i]),
                slope * lsk,
            ]
            parts = [prob * lab, prob, lab, lsk * prob, lsk] + fields
            for n, v in enumerate(parts):
                sums[n] = sums[n] + v
            for f, v in enumerate(fields):
                x_ref[0, f, o + i] = v
                high = v.astype(jnp.bfloat16)
                low = (v - high.astype(jnp.float32)).astype(jnp.bfloat16)
                for t in range(height // 16):
                    at = pl.ds(pl.multiple_of((k * FIELDS + f) * 32, 32), 16)
                    S[o + i, at, t * wd : (t + 1) * wd] = high[16 * t : 16 * t + 16]
                    at = pl.ds(pl.multiple_of((k * FIELDS + f) * 32, 32) + 16, 16)
                    S[o + i, at, t * wd : (t + 1) * wd] = low[16 * t : 16 * t + 16]

    sweep(HALO, HALO + depth, last)
    tp, sp, sl, lsp, ls = sums[:5]

    def stack(values):
        values = [jnp.sum(v, axis=0, keepdims=True) for v in values]
        values += [jnp.zeros((1, wd), jnp.float32)] * (8 - len(values))
        return jnp.concatenate(values, axis=0)

    col = lax.broadcasted_iota(jnp.int32, (wd, wd // 4), 1)

    def column(n):
        return jnp.where(col == n, 1.0, 0.0)

    here = jnp.dot(stack([tp, sp, sl, sky, sk, lsp, ls]), column(k), precision=EXACT)
    here = here + jnp.dot(stack(sums[5:]), column(pl.num_programs(0) + k), precision=EXACT)

    @pl.when(k == 0)
    def _():
        T[...] = here

    @pl.when(k > 0)
    def _():
        T[...] = T[...] + here

    @pl.when(k == pl.num_programs(0) - 1)
    def _():
        channels = f_ref.shape[0]
        cols = S.shape[1]

        def plane(d, carry):
            f = jnp.concatenate(
                [f_ref[:, d, 16 * t : 16 * t + 16, :].reshape(channels * 16, wd) for t in range(height // 16)],
                axis=1,
            )
            got = lax.dot_general(f, S[d], LAST, preferred_element_type=jnp.float32)

            @pl.when(d == 0)
            def _():
                A[...] = got

            @pl.when(d > 0)
            def _():
                A[...] = A[...] + got

            return carry

        lax.fori_loop(0, depth, plane, 0)
        h = lax.broadcasted_iota(jnp.int32, (channels, 16, cols), 1)
        g = lax.broadcasted_iota(jnp.int32, (channels, 16, cols), 2) % 16
        m = jnp.sum(jnp.where(h == g, A[...].reshape(channels, 16, cols), 0.0), axis=1)
        item = lax.broadcasted_iota(jnp.int32, (8, cols), 0)
        at = lax.broadcasted_iota(jnp.int32, (8, cols), 1) // 32
        heads = []
        for n in range(cols // 32 // FIELDS):
            pick = jnp.where((at == n * FIELDS + item) & (item < FIELDS), 1.0, 0.0)
            heads.append(lax.dot_general(pick, m, LAST, precision=EXACT))
        whole = jnp.concatenate(heads + [T[...]], axis=1)
        for n in range(sum_ref.shape[0]):
            sum_ref[n] = whole


def run_core(copies, features, own, lo, hi, left, right, labels, prob, lsk):
    classes, depth, height, wd = prob.shape
    channels = features.shape[0]
    planes = depth + 2 * HALO
    lplanes = depth + 2 * LHALO
    args = (own, lo, hi, left, right, labels, prob, lsk)
    n = ITERS + 1
    cols = classes * FIELDS * 32
    fields = jax.ShapeDtypeStruct((classes, FIELDS, depth, height, wd), jnp.float32)
    sums = jax.ShapeDtypeStruct((copies, 8, wd), jnp.float32)
    return pl.pallas_call(
        core_kernel,
        grid=(classes,),
        in_specs=[pl.BlockSpec(features.shape, lambda k: (0, 0, 0, 0))] + [by_class(v) for v in args],
        out_specs=[by_class(fields), pl.BlockSpec(sums.shape, lambda k: (0, 0, 0))],
        out_shape=[fields, sums],
        scratch_shapes=[
            pltpu.VMEM((n + 1, planes, ROWS, wd), jnp.float32),
            pltpu.VMEM((n, planes, ROWS, wd), jnp.float32),
            pltpu.VMEM((n, lplanes, ROWS, wd), jnp.float32),
            pltpu.VMEM((n, lplanes, ROWS, wd), jnp.float32),
            pltpu.VMEM((n, lplanes, ROWS, wd), jnp.float32),
            pltpu.VMEM((2, 2, lplanes, ROWS, wd), jnp.float32),
            pltpu.VMEM((lplanes, ROWS, wd), jnp.float32),
            pltpu.VMEM((depth, cols, height // 16 * wd), jnp.bfloat16),
            pltpu.VMEM((channels * 16, cols), jnp.float32),
            pltpu.VMEM((8, wd // 4), jnp.float32),
            pltpu.VMEM((2 * wd, wd), jnp.bfloat16),
        ],
        compiler_params=pltpu.CompilerParams(vmem_limit_bytes=60 * 2**20),
        name="core",
    )(features, *args)


def tail_kernel(cells, w_ref, s_ref, x_ref, g_ref, out_ref, C):
    classes = x_ref.shape[0]
    channels = g_ref.shape[0]
    quarter = s_ref.shape[2] // 4
    wd = s_ref.shape[2]

    @pl.when(pl.program_id(0) == 0)
    def _():
        total = jnp.sum(s_ref[...], axis=0)
        tp, sp, sl, sky, sk, lsp, ls = [jnp.broadcast_to(total[i : i + 1], total.shape) for i in range(7)]
        prec = (sky + 1.0) / (sk + 1.0)
        sens = (lsp + 1.0) / (ls + 1.0)
        both = prec + sens
        cldice = 1.0 - 2.0 * prec * sens / both
        bottom = tp + ALPHA * (sp - tp) + BETA * (sl - tp) + 1.0
        tversky = (tp + 1.0) / bottom
        term = cldice + 1.0 - tversky
        scale = cells / classes
        by_prec = -2.0 * (sens / both) * (sens / both) * scale
        by_sens = -2.0 * (prec / both) * (prec / both) * scale
        by_sky = by_prec / (sk + 1.0)
        by_sk = -by_sky * prec
        by_lsp = by_sens / (ls + 1.0)
        by_sp = scale * ALPHA * tversky / bottom
        by_tp = scale * (tversky * (1.0 - ALPHA - BETA) - 1.0) / bottom
        lane = lax.broadcasted_iota(jnp.int32, total.shape, 1)
        item = lax.broadcasted_iota(jnp.int32, total.shape, 0)
        mult = jnp.zeros_like(total)
        loss = jnp.zeros_like(total)
        for k in range(classes):
            mine = (lane // quarter == k) | (lane == classes * (quarter + 1) + k)
            spot = lane == classes * quarter + k

            def pick(v):
                return jnp.sum(jnp.where(spot, v, 0.0), axis=1, keepdims=True)

            for f, v in enumerate((by_tp, by_sp, by_sky, by_sk, by_lsp)):
                v = jnp.broadcast_to(pick(v), total.shape)
                C[k, f] = v
                mult = jnp.where(mine & (item == f), v, mult)
            loss = loss + pick(term) * (1.0 / classes)
        grad = jnp.sum(jnp.where(item < FIELDS, total * mult, 0.0), axis=0, keepdims=True)
        square = jnp.sum(grad * grad, axis=1, keepdims=True)
        rms = jnp.sqrt(square / (classes * channels + classes) + 1e-06)
        out_ref[...] = jnp.where(item == 0, grad / rms, loss)

    height = x_ref.shape[3]
    for p in range(x_ref.shape[2]):
        for t in range(height // 16):
            rows = slice(16 * t, 16 * t + 16)
            dlogit = []
            for k in range(classes):
                v = None
                for f in range(FIELDS):
                    c = jnp.concatenate([C[k, f]] * 2, axis=0)
                    term = c * x_ref[k, f, p, rows, :]
                    v = term if v is None else v + term
                dlogit.append(v)
            for c in range(channels):
                v = None
                for k in range(classes):
                    term = w_ref[k, c] * dlogit[k]
                    v = term if v is None else v + term
                g_ref[c, p, rows, :] = v.astype(jnp.bfloat16)


def run_tail(cells, weight, sums, fields):
    classes, n, depth, height, wd = fields.shape
    channels = weight.shape[1]
    step = 2
    return pl.pallas_call(
        functools.partial(tail_kernel, cells),
        grid=(depth // step,),
        in_specs=[
            pl.BlockSpec(memory_space=pltpu.SMEM),
            pl.BlockSpec(sums.shape, lambda d: (0, 0, 0)),
            pl.BlockSpec((classes, n, step, height, wd), lambda d: (0, 0, d, 0, 0)),
        ],
        out_specs=[
            pl.BlockSpec((channels, step, height, wd), lambda d: (0, d, 0, 0)),
            pl.BlockSpec((8, wd), lambda d: (0, 0)),
        ],
        out_shape=[
            jax.ShapeDtypeStruct((channels, depth, height, wd), jnp.bfloat16),
            jax.ShapeDtypeStruct((8, wd), jnp.float32),
        ],
        scratch_shapes=[pltpu.VMEM((classes, FIELDS, 8, wd), jnp.float32)],
        compiler_params=pltpu.CompilerParams(vmem_limit_bytes=32 * 2**20),
        name="tail",
    )(weight, sums, fields)


def per_device(features, head_weight, head_bias, labels, label_skeleton):
    classes, channels = head_weight.shape
    _, block_d, block_h, wd = features.shape
    cells = block_d * lax.axis_size("depth") * block_h * lax.axis_size("height") * wd
    weight = head_weight.astype(jnp.float32)
    prob, own, first, last = run_head(weight, head_bias, features, labels)
    lo, hi = shift(last, "depth", 1), shift(first, "depth", -1)
    first, last = run_side(own, labels, lo, hi)
    left, right = shift(last, "height", 1), shift(first, "height", -1)
    fields, local = run_core(
        lax.axis_size("height"), features, own, lo, hi, left, right, labels, prob, label_skeleton
    )
    part = jnp.sum(lax.all_to_all(local, "height", 0, 0, tiled=True), axis=0)
    spread = jnp.broadcast_to(part[None], (lax.axis_size("depth"),) + part.shape)
    parts = lax.all_to_all(spread, "depth", 0, 0, tiled=True)
    grad_features, small = run_tail(cells, weight, parts, fields)
    n = classes * channels
    return (
        small[1, 0],
        grad_features,
        small[0, :n].reshape(classes, channels),
        small[0, n + classes : n + 2 * classes],
    )


def solution(mesh):
    return jax.shard_map(
        per_device,
        mesh=mesh,
        in_specs=(
            P(None, "depth", "height", None),
            P(),
            P(),
            P(None, "depth", "height", None),
            P(None, "depth", "height", None),
        ),
        out_specs=(P(), P(None, "depth", "height", None), P(), P()),
        check_vma=False,
    )
```

```python
import functools

import jax
import jax.numpy as jnp
from jax import lax
from jax.experimental import pallas as pl
from jax.experimental.pallas import tpu as pltpu
from jax.sharding import PartitionSpec as P

ITERS = 3
TAU = 0.1
SHARP = 0.05
ALPHA = 0.3
BETA = 0.7
HALO = 10
LHALO = 5
ROWS = 80
OFF = 24
NB = 4
MXU = 4
CHUNK = 4
FIELDS = 5
EARLY = 3
EXACT = lax.Precision.HIGHEST
LAST = (((1,), (1,)), ((), ()))


def shift(value, axis, step):
    n = lax.axis_size(axis)
    pairs = [(i, i + step) for i in range(n) if 0 <= i + step < n]
    return lax.ppermute(value, axis, pairs)


def head_kernel(w_hbm, b_hbm, f_hbm, l_hbm, p_ref, e_ref, first_ref, last_ref, spread_ref, F, L, W, B, sems):
    channels, depth, height, wd = F.shape
    classes = p_ref.shape[0]
    small = [
        pltpu.make_async_copy(w_hbm, W, sems.at[depth]),
        pltpu.make_async_copy(b_hbm, B, sems.at[depth + 1]),
    ]
    edges = [
        pltpu.make_async_copy(l_hbm.at[:, 0:LHALO], L.at[0], sems.at[depth + 2]),
        pltpu.make_async_copy(l_hbm.at[:, depth - LHALO : depth], L.at[1], sems.at[depth + 3]),
    ]
    planes = [
        pltpu.make_async_copy(f_hbm.at[:, d], F.at[:, d], sems.at[d]) for d in range(depth)
    ]
    for copy in small + planes + edges:
        copy.start()
    for copy in small:
        copy.wait()
    weight = W[...].astype(jnp.float32)
    for k in range(classes):
        for c in range(channels):
            spread_ref[k, c : c + 1, :] = jnp.broadcast_to(weight[k : k + 1, c : c + 1], (1, wd))
    bias = [jnp.broadcast_to(B[0:1, k : k + 1], (height, wd)) for k in range(classes)]
    for d in range(depth):
        planes[d].wait()
        acc = [None] * classes
        for c in range(channels):
            f = F[c, d].astype(jnp.float32)
            for k in range(classes):
                term = jnp.broadcast_to(spread_ref[k, c : c + 1, :], (height, wd)) * f
                acc[k] = term if c == 0 else acc[k] + term
        for k in range(classes):
            prob = 1.0 / (1.0 + jnp.exp(-(acc[k] + bias[k])))
            p_ref[k, d] = prob
            e = jnp.exp(prob * (-1.0 / TAU))
            e_ref[k, d] = e
            if d < HALO:
                first_ref[k, d * height : (d + 1) * height, :] = e
            if d >= depth - HALO:
                at = (d - (depth - HALO)) * height
                last_ref[k, at : at + height, :] = e
    for copy, n, out in zip(edges, range(2), (first_ref, last_ref)):
        copy.wait()
        for k in range(classes):
            for p in range(LHALO):
                at = (HALO + p) * height
                out[k, at : at + height, :] = L[n, k, p].astype(jnp.float32)


VMEM = pl.BlockSpec(memory_space=pltpu.VMEM)
HBM = pl.BlockSpec(memory_space=pltpu.HBM)


def run_head(weight, bias, features, labels):
    classes, channels = weight.shape
    depth, height, wd = features.shape[1:]
    full = jax.ShapeDtypeStruct((classes, depth, height, wd), jnp.float32)
    edge = jax.ShapeDtypeStruct((classes, (HALO + LHALO) * height, wd), jnp.float32)
    return pl.pallas_call(
        head_kernel,
        in_specs=[HBM] * 4,
        out_specs=[VMEM] * 5,
        out_shape=[full, full, edge, edge, jax.ShapeDtypeStruct((classes, channels, wd), jnp.float32)],
        scratch_shapes=[
            pltpu.VMEM(features.shape, features.dtype),
            pltpu.VMEM((2, classes, LHALO, height, wd), jnp.int32),
            pltpu.VMEM(weight.shape, weight.dtype),
            pltpu.VMEM((1, classes), jnp.float32),
            pltpu.SemaphoreType.DMA((depth + 4,)),
        ],
        compiler_params=pltpu.CompilerParams(vmem_limit_bytes=62 * 2**20),
        name="head",
    )(weight, bias.reshape(1, classes), features, labels)


def side_kernel(own_ref, lab_ref, lo_ref, hi_ref, first_ref, last_ref):
    classes, depth, height = own_ref.shape[:3]
    for k in range(classes):
        for out, near in ((first_ref, True), (last_ref, False)):
            base, skip = 0, 0
            for ref, width in ((own_ref, HALO), (lab_ref, LHALO)):
                at = 0 if near else height - width
                for p in range(depth + 2 * width):
                    if p < width:
                        v = lo_ref[k, pl.ds((skip + p) * height + at, width), :]
                    elif p < width + depth:
                        v = ref[k, p - width, pl.ds(at, width), :].astype(jnp.float32)
                    else:
                        v = hi_ref[k, pl.ds((skip + p - width - depth) * height + at, width), :]
                    out[k, pl.ds(base + p * width, width), :] = v
                base += width * (depth + 2 * width)
                skip += width


def run_side(own, labels, lo, hi):
    classes, depth, height, wd = own.shape
    rows = HALO * (depth + 2 * HALO) + LHALO * (depth + 2 * LHALO)
    edge = jax.ShapeDtypeStruct((classes, rows, wd), jnp.float32)
    return pl.pallas_call(
        side_kernel,
        in_specs=[VMEM] * 4,
        out_specs=[VMEM] * 2,
        out_shape=[edge, edge],
        compiler_params=pltpu.CompilerParams(vmem_limit_bytes=16 * 2**20),
        name="side",
    )(own, labels, lo, hi)


def stash(S, group, plane, value):
    height, wd = value.shape
    high = value.astype(jnp.bfloat16)
    low = (value - high.astype(jnp.float32)).astype(jnp.bfloat16)
    for t in range(height // 16):
        at = (plane * (height // 16) + t) * wd
        S[32 * group : 32 * group + 16, at : at + wd] = high[16 * t : 16 * t + 16]
        S[32 * group + 16 : 32 * group + 32, at : at + wd] = low[16 * t : 16 * t + 16]


def contract(f_ref, S):
    channels, depth, height, wd = f_ref.shape
    cols = S.shape[0]
    total = None
    for d in range(0, depth, CHUNK):
        f = jnp.concatenate(
            [
                f_ref[:, d + i, 16 * t : 16 * t + 16, :].reshape(channels * 16, wd)
                for i in range(CHUNK)
                for t in range(height // 16)
            ],
            axis=1,
        )
        n = height // 16 * wd
        got = lax.dot_general(f, S[:, d * n : (d + CHUNK) * n], LAST, preferred_element_type=jnp.float32)
        total = got if total is None else total + got
    h = lax.broadcasted_iota(jnp.int32, (channels, 16, cols), 1)
    g = lax.broadcasted_iota(jnp.int32, (channels, 16, cols), 2) % 16
    return jnp.sum(jnp.where(h == g, total.reshape(channels, 16, cols), 0.0), axis=1)


def collect(m, fields):
    cols = m.shape[1]
    item = lax.broadcasted_iota(jnp.int32, (8, cols), 0)
    at = lax.broadcasted_iota(jnp.int32, (8, cols), 1) // 32
    pick = jnp.zeros((8, cols), jnp.float32)
    for row, group in enumerate(fields):
        if group is not None:
            pick = jnp.where((item == row) & (at == group), 1.0, pick)
    return lax.dot_general(pick, m, LAST, precision=EXACT)


def by_rows(values, lane):
    wd = next(v for v in values if v is not None).shape[1]
    values = [jnp.zeros((1, wd), jnp.float32) if v is None else jnp.sum(v, axis=0, keepdims=True) for v in values]
    values += [jnp.zeros((1, wd), jnp.float32)] * (8 - len(values))
    col = lax.broadcasted_iota(jnp.int32, (wd, wd // 4), 1)
    return jnp.dot(jnp.concatenate(values, axis=0), jnp.where(col == lane, 1.0, 0.0), precision=EXACT)


def early_kernel(f_ref, l_ref, p_ref, k_ref, sum_ref, S):
    classes, depth, height, wd = p_ref.shape
    parts = None
    for k in range(classes):
        sums = [None] * 8
        for d in range(depth):
            prob = p_ref[k, d]
            lab = l_ref[k, d].astype(jnp.float32)
            lsk = k_ref[k, d].astype(jnp.float32)
            slope = prob * (1.0 - prob)
            fields = [slope * lab, slope, slope * lsk]
            for n, v in enumerate([prob * lab, prob, lab, lsk * prob, lsk] + fields):
                sums[n] = v if sums[n] is None else sums[n] + v
            for f, v in enumerate(fields):
                stash(S, k * EARLY + f, d, v)
        here = by_rows(sums[:3] + [None, None] + sums[3:5], k) + by_rows(sums[5:], classes + k)
        parts = here if parts is None else parts + here
    m = contract(f_ref, S)
    heads = [collect(m, [k * EARLY + f for f in range(EARLY)]) for k in range(classes)]
    sum_ref[...] = jnp.concatenate(heads + [parts], axis=1)


def run_early(features, labels, prob, lsk):
    classes, depth, height, wd = prob.shape
    return pl.pallas_call(
        early_kernel,
        in_specs=[VMEM] * 4,
        out_specs=VMEM,
        out_shape=jax.ShapeDtypeStruct((8, wd), jnp.float32),
        scratch_shapes=[pltpu.VMEM((classes * EARLY * 32, depth * (height // 16) * wd), jnp.bfloat16)],
        compiler_params=pltpu.CompilerParams(vmem_limit_bytes=24 * 2**20),
        cost_estimate=pl.CostEstimate(flops=10**9, bytes_accessed=10**7, transcendentals=0),
        name="early",
    )(features, labels, prob, lsk)


def wide_sums(values, lane, band):
    rows, width = values[0].shape
    out = []
    if MXU:
        s = jnp.concatenate(values[:MXU], axis=0)
        high = s.astype(jnp.bfloat16)
        low = (s - high.astype(jnp.float32)).astype(jnp.bfloat16)
        s = jnp.dot(jnp.concatenate([high, low], axis=1), band, preferred_element_type=jnp.float32)
        out = [s[i * rows : (i + 1) * rows] for i in range(MXU)]
    for s in values[MXU:]:
        left = jnp.where(lane == 0, 0.0, pltpu.roll(s, 1, 1))
        right = jnp.where(lane == width - 1, 0.0, pltpu.roll(s, width - 1, 1))
        out.append(s + left + right)
    return out


def boxes(load, d, r0, nr, lane, band):
    h = []
    for i in range(NB + 2):
        h.append(load(d + i - 1, r0 - 1, nr) + load(d + i - 1, r0, nr) + load(d + i - 1, r0 + 1, nr))
    out = []
    for i in range(0, NB, 2):
        mid = h[i + 1] + h[i + 2]
        out.append(h[i] + mid)
        out.append(mid + h[i + 3])
    return wide_sums(out, lane, band)


def sweep(first, last, body):
    for i in range(first, last, NB):
        body(min(i, last - NB))


def core_kernel(
    k, classes,
    before_ref, f_ref, e_own, lo, hi, left, right, l_own, p_own, k_own,
    x_ref, sum_ref,
    E, R, X, U, V, Q, L, S,
):
    depth, height, wd = p_own.shape[1:]
    planes = depth + 2 * HALO
    lplanes = depth + 2 * LHALO
    base = HALO - LHALO

    row = lax.broadcasted_iota(jnp.int32, (2 * wd, wd), 0)
    col = lax.broadcasted_iota(jnp.int32, (2 * wd, wd), 1)
    near = jnp.abs(jnp.where(row < wd, row, row - wd) - col) <= 1
    band = jnp.where(near, 1.0, 0.0).astype(jnp.bfloat16)

    E[0, :, OFF - HALO - 8 : OFF - HALO, :] = jnp.zeros((planes, 8, wd), jnp.float32)
    E[0, :, OFF + height + HALO : OFF + height + HALO + 8, :] = jnp.zeros((planes, 8, wd), jnp.float32)
    L[:, OFF - 8 : OFF - LHALO, :] = jnp.zeros((lplanes, 8 - LHALO, wd), jnp.float32)
    L[:, OFF + height + LHALO : OFF + height + 8, :] = jnp.zeros((lplanes, 8 - LHALO, wd), jnp.float32)

    def gather(put, width, own, skip, base):
        put(slice(width, width + depth), slice(OFF, OFF + height), own[k])
        for p in range(width):
            rows = slice((skip + p) * height, (skip + p + 1) * height)
            put(p, slice(OFF, OFF + height), lo[k, rows, :])
            put(width + depth + p, slice(OFF, OFF + height), hi[k, rows, :])
        for p in range(depth + 2 * width):
            rows = slice(base + p * width, base + (p + 1) * width)
            put(p, slice(OFF - width, OFF), left[k, rows, :])
            put(p, slice(OFF + height, OFF + height + width), right[k, rows, :])

    def put_e(p, rows, v):
        E[0, p, rows, :] = v

    def put_l(p, rows, v):
        L[p, rows, :] = v.astype(jnp.float32)

    gather(put_e, HALO, e_own, 0, 0)
    gather(put_l, LHALO, l_own, HALO, HALO * planes)
    w0, wn = OFF - 8, height + 16
    lane = lax.broadcasted_iota(jnp.int32, (wn, wd), 1)
    lane_big = lax.broadcasted_iota(jnp.int32, (wn + 16, wd), 1)
    lane_own = lax.broadcasted_iota(jnp.int32, (height, wd), 1)

    for j in range(ITERS + 1):
        r0, nr, ln = (w0 - 8, wn + 16, lane_big) if j == 0 else (w0, wn, lane)

        def erode(d, j=j, r0=r0, nr=nr, ln=ln):
            outs = boxes(lambda a, b, n: E[j, a, pl.ds(b, n), :], d, r0, nr, ln, band)
            for i, s in enumerate(outs):
                live = E[0, d + i, pl.ds(r0, nr), :] > 0.0
                E[j + 1, d + i, pl.ds(r0, nr), :] = jnp.where(live, s, 0.0)
                R[j, d + i, pl.ds(r0, nr), :] = jnp.where(live, 1.0 / s, 0.0)

        sweep(j + 1, planes - j - 1, erode)

    for j in range(ITERS + 1):

        def dilate(d, j=j):
            outs = boxes(lambda a, b, n: R[j, a, pl.ds(b, n), :], d, w0, wn, lane, band)
            for i, s in enumerate(outs):
                live = E[0, d + i, pl.ds(w0, wn), :] > 0.0
                rd = 1.0 / s
                t = rd * R[j - 1, d + i, pl.ds(w0, wn), :] if j else rd / E[0, d + i, pl.ds(w0, wn), :]
                U[j, d + i - base, pl.ds(w0, wn), :] = jnp.where(live, rd, 0.0)
                X[j, d + i - base, pl.ds(w0, wn), :] = jnp.where(live, t * t, 0.0)

        sweep(base, planes - base, dilate)

    row = lax.broadcasted_iota(jnp.int32, (wn, wd), 0)
    inner = jnp.where((row >= OFF - w0) & (row < OFF - w0 + height), 1.0, 0.0)

    def point(d, carry):
        rows = pl.ds(w0, wn)
        x = [X[j, d, rows, :] for j in range(ITERS + 1)]
        opx = [1.0 + v for v in x]
        logs = [jnp.log(v) for v in opx]
        skel = SHARP * logs[0]
        om, e, ope = [None], [None], [None]
        for j in range(1, ITERS + 1):
            om.append(1.0 - skel)
            e.append(jnp.exp(logs[j] * om[j]))
            ope.append(1.0 + e[j])
            skel = skel + SHARP * jnp.log(ope[j])
        lab = L[d, rows, :]
        g = None
        for j in range(ITERS, -1, -1):
            if j:
                both = 1.0 / (opx[j] * ope[j])
                gv = x[j] * e[j] * om[j] * both
                keep = 1.0 - (SHARP * logs[j]) * (e[j] * opx[j] * both)
            else:
                gv = x[0] / opx[0]
            if g is not None:
                gv = gv * g
            if j:
                g = keep if g is None else g * keep
            u = gv * U[j, d, rows, :]
            X[j, d, rows, :] = gv
            U[j, d, rows, :] = u
            V[j, d, rows, :] = u * lab
        own = jnp.where((d >= LHALO) & (d < LHALO + depth), 1.0, 0.0)
        skel = skel * (inner * own)
        return carry[0] + skel * lab, carry[1] + skel

    zero = jnp.zeros((wn, wd), jnp.float32)
    sky, sk = lax.fori_loop(0, lplanes, point, (zero, zero), unroll=2)

    for j in range(ITERS + 1, 0, -1):
        now, nxt = j % 2, (j + 1) % 2

        def back(d, j=j, now=now, nxt=nxt):
            b = d - base
            for which, src in ((0, V), (1, U)):
                du = boxes(lambda a, c, n: src[j - 1, a, pl.ds(c, n), :], b, w0, wn, lane, band)
                if j <= ITERS:
                    dq = boxes(lambda a, c, n: Q[which, nxt, a, pl.ds(c, n), :], b, w0, wn, lane, band)
                for i in range(NB):
                    r = R[j - 1, d + i, pl.ds(w0, wn), :]
                    v = -r * du[i]
                    if j <= ITERS:
                        live = E[0, d + i, pl.ds(w0, wn), :] > 0.0
                        gv = X[j, b + i, pl.ds(w0, wn), :]
                        if which == 0:
                            gv = gv * L[b + i, pl.ds(w0, wn), :]
                        v = jnp.where(live, r * (gv + v) + dq[i], 0.0)
                    else:
                        v = r * v
                    Q[which, now, b + i, pl.ds(w0, wn), :] = v

        sweep(HALO - j, planes - HALO + j, back)

    sums = [jnp.zeros((height, wd), jnp.float32) for _ in range(FIELDS - EARLY)]

    def last(d):
        b = d - base
        o = d - HALO
        grads = [
            boxes(lambda a, c, n: Q[which, 1, a, pl.ds(c, n), :], b, OFF, height, lane_own, band)
            for which in range(2)
        ]
        for i in range(NB):
            e = E[0, d + i, pl.ds(OFF, height), :]
            gv = X[0, b + i, pl.ds(OFF, height), :]
            prob = p_own[k, o + i]
            lab = L[b + i, pl.ds(OFF, height), :]
            slope = prob * (1.0 - prob)
            fields = [slope * (gv * lab + e * grads[0][i]), slope * (gv + e * grads[1][i])]
            for f, v in enumerate(fields):
                sums[f] = sums[f] + v
                x_ref[2 + f, o + i] = v
                stash(S, f, o + i, v)
            x_ref[0, o + i] = slope
            x_ref[1, o + i] = lab + 2.0 * k_own[k, o + i].astype(jnp.float32)

    sweep(HALO, HALO + depth, last)
    parts = by_rows([None] * 3 + [sky, sk], k) + by_rows([None] * EARLY + sums, classes + k)
    heads = collect(contract(f_ref, S), [None] * EARLY + [0, 1])
    blank = jnp.zeros_like(heads)
    whole = jnp.concatenate([heads if n == k else blank for n in range(classes)] + [parts], axis=1)
    whole = whole + before_ref[...]
    for n in range(sum_ref.shape[0]):
        sum_ref[n] = whole


def run_core(k, copies, before, features, own, near, labels, prob, lsk):
    classes, depth, height, wd = prob.shape
    planes = depth + 2 * HALO
    lplanes = depth + 2 * LHALO
    args = (before, features, own, *near, labels, prob, lsk)
    n = ITERS + 1
    fields = jax.ShapeDtypeStruct((4, depth, height, wd), jnp.float32)
    sums = jax.ShapeDtypeStruct((copies, 8, wd), jnp.float32)
    return pl.pallas_call(
        functools.partial(core_kernel, k, classes),
        in_specs=[VMEM] * len(args),
        out_specs=[VMEM] * 2,
        out_shape=[fields, sums],
        scratch_shapes=[
            pltpu.VMEM((n + 1, planes, ROWS, wd), jnp.float32),
            pltpu.VMEM((n, planes, ROWS, wd), jnp.float32),
            pltpu.VMEM((n, lplanes, ROWS, wd), jnp.float32),
            pltpu.VMEM((n, lplanes, ROWS, wd), jnp.float32),
            pltpu.VMEM((n, lplanes, ROWS, wd), jnp.float32),
            pltpu.VMEM((2, 2, lplanes, ROWS, wd), jnp.float32),
            pltpu.VMEM((lplanes, ROWS, wd), jnp.float32),
            pltpu.VMEM(((FIELDS - EARLY) * 32, depth * (height // 16) * wd), jnp.bfloat16),
        ],
        compiler_params=pltpu.CompilerParams(vmem_limit_bytes=34 * 2**20),
        cost_estimate=pl.CostEstimate(flops=2 * 10**10, bytes_accessed=4 * 10**7, transcendentals=0),
        name=f"core{k}",
    )(*args)


def tail_kernel(cells, w_ref, s_ref, *refs):
    classes = len(refs) - 5
    x_ref = refs[:classes]
    g_ref, loss_ref, gw_ref, gb_ref, C = refs[classes:]
    channels = g_ref.shape[0]
    quarter = s_ref.shape[2] // 4
    wd = s_ref.shape[2]

    @pl.when(pl.program_id(0) == 0)
    def _():
        total = jnp.sum(s_ref[...], axis=0)
        tp, sp, sl, sky, sk, lsp, ls = [jnp.broadcast_to(total[i : i + 1], total.shape) for i in range(7)]
        prec = (sky + 1.0) / (sk + 1.0)
        sens = (lsp + 1.0) / (ls + 1.0)
        both = prec + sens
        cldice = 1.0 - 2.0 * prec * sens / both
        bottom = tp + ALPHA * (sp - tp) + BETA * (sl - tp) + 1.0
        tversky = (tp + 1.0) / bottom
        term = cldice + 1.0 - tversky
        scale = cells / classes
        by_prec = -2.0 * (sens / both) * (sens / both) * scale
        by_sens = -2.0 * (prec / both) * (prec / both) * scale
        by_sky = by_prec / (sk + 1.0)
        by_sk = -by_sky * prec
        by_lsp = by_sens / (ls + 1.0)
        by_sp = scale * ALPHA * tversky / bottom
        by_tp = scale * (tversky * (1.0 - ALPHA - BETA) - 1.0) / bottom
        lane = lax.broadcasted_iota(jnp.int32, total.shape, 1)
        item = lax.broadcasted_iota(jnp.int32, total.shape, 0)
        mult = jnp.zeros_like(total)
        loss = jnp.zeros_like(total)
        for k in range(classes):
            mine = (lane // quarter == k) | (lane == classes * (quarter + 1) + k)
            spot = lane == classes * quarter + k

            def pick(v):
                return jnp.sum(jnp.where(spot, v, 0.0), axis=1, keepdims=True)

            for f, v in enumerate((by_tp, by_sp, by_lsp, by_sky, by_sk)):
                v = jnp.broadcast_to(pick(v), total.shape)
                C[k, f] = v
                mult = jnp.where(mine & (item == f), v, mult)
            loss = loss + pick(term) * (1.0 / classes)
        grad = jnp.sum(jnp.where(item < FIELDS, total * mult, 0.0), axis=0, keepdims=True)
        square = jnp.sum(grad * grad, axis=1, keepdims=True)
        rms = jnp.sqrt(square / (classes * channels + classes) + 1e-06)
        grad = grad / rms
        loss_ref[...] = loss[0:1, 0:1]
        gw_ref[...] = jnp.concatenate([grad[:, k * quarter : (k + 1) * quarter] for k in range(classes)], axis=0)
        n = classes * (quarter + 1)
        gb_ref[...] = grad[:, n : n + classes]

    height = g_ref.shape[2]
    base = pl.program_id(0) * g_ref.shape[1]
    for p in range(g_ref.shape[1]):
        for t in range(height // 16):
            rows = slice(16 * t, 16 * t + 16)
            dlogit = []
            for k in range(classes):
                c = [jnp.concatenate([C[k, f]] * 2, axis=0) for f in range(FIELDS)]
                slope, code, ga, gb = [x_ref[k][f, base + p, rows, :] for f in range(4)]
                lsk = code >= 2.0
                lab = jnp.where(lsk, code - 2.0, code)
                v = slope * (c[0] * lab + c[1] + jnp.where(lsk, c[2], 0.0)) + c[3] * ga + c[4] * gb
                dlogit.append(v)
            for c in range(channels):
                v = None
                for k in range(classes):
                    term = jnp.broadcast_to(w_ref[k, c : c + 1, :], (16, wd)) * dlogit[k]
                    v = term if v is None else v + term
                g_ref[c, p, rows, :] = v.astype(jnp.bfloat16)


def run_tail(cells, spread, sums, fields):
    depth, height, wd = fields[0].shape[1:]
    classes, channels = spread.shape[:2]
    step = 2
    return pl.pallas_call(
        functools.partial(tail_kernel, cells),
        grid=(depth // step,),
        in_specs=[VMEM] * (2 + classes),
        out_specs=[
            pl.BlockSpec((channels, step, height, wd), lambda d: (0, d, 0, 0)),
            pl.BlockSpec((1, 1), lambda d: (0, 0)),
            pl.BlockSpec((classes, channels), lambda d: (0, 0)),
            pl.BlockSpec((1, classes), lambda d: (0, 0)),
        ],
        out_shape=[
            jax.ShapeDtypeStruct((channels, depth, height, wd), jnp.bfloat16),
            jax.ShapeDtypeStruct((1, 1), jnp.float32),
            jax.ShapeDtypeStruct((classes, channels), jnp.float32),
            jax.ShapeDtypeStruct((1, classes), jnp.float32),
        ],
        scratch_shapes=[pltpu.VMEM((classes, FIELDS, 8, wd), jnp.float32)],
        compiler_params=pltpu.CompilerParams(vmem_limit_bytes=16 * 2**20),
        name="tail",
    )(spread, sums, *fields)


def per_device(features, head_weight, head_bias, labels, label_skeleton):
    classes, channels = head_weight.shape
    _, block_d, block_h, wd = features.shape
    cells = block_d * lax.axis_size("depth") * block_h * lax.axis_size("height") * wd
    prob, own, first, last, spread = run_head(head_weight, head_bias, features, labels)
    lo, hi = shift(last, "depth", 1), shift(first, "depth", -1)
    local = run_early(features, labels, prob, label_skeleton)
    lo, hi, local = lax.optimization_barrier((lo, hi, local))
    first, last = run_side(own, labels, lo, hi)
    near = (lo, hi, shift(last, "height", 1), shift(first, "height", -1))
    fields = []
    for k in range(classes):
        copies = lax.axis_size("height") if k == classes - 1 else 1
        mine, local = run_core(k, copies, local, features, own, near, labels, prob, label_skeleton)
        fields.append(mine)
        if copies == 1:
            local = local[0]
    part = jnp.sum(lax.all_to_all(local, "height", 0, 0, tiled=True), axis=0)
    part = jnp.broadcast_to(part[None], (lax.axis_size("depth"),) + part.shape)
    parts = lax.all_to_all(part, "depth", 0, 0, tiled=True)
    grad_features, loss, grad_w, grad_b = run_tail(cells, spread, parts, fields)
    return loss[0, 0], grad_features, grad_w, grad_b[0]


def solution(mesh):
    return jax.shard_map(
        per_device,
        mesh=mesh,
        in_specs=(
            P(None, "depth", "height", None),
            P(),
            P(),
            P(None, "depth", "height", None),
            P(None, "depth", "height", None),
        ),
        out_specs=(P(), P(None, "depth", "height", None), P(), P()),
        check_vma=False,
    )
```

```python
import functools

import jax
import jax.numpy as jnp
from jax import lax
from jax.experimental import pallas as pl
from jax.experimental.pallas import tpu as pltpu
from jax.sharding import PartitionSpec as P

ITERS = 3
TAU = 0.1
SHARP = 0.05
ALPHA = 0.3
BETA = 0.7
HALO = 10
LHALO = 5
ROWS = 80
OFF = 24
NB = 4
MXU = 4
CHUNK = 4
FIELDS = 5
EARLY = 3
EXACT = lax.Precision.HIGHEST
LAST = (((1,), (1,)), ((), ()))


def shift(value, axis, step):
    n = lax.axis_size(axis)
    pairs = [(i, i + step) for i in range(n) if 0 <= i + step < n]
    return lax.ppermute(value, axis, pairs)


def head_kernel(w_hbm, b_hbm, f_hbm, l_hbm, p_ref, e_ref, first_ref, last_ref, spread_ref, F, L, W, B, sems):
    channels, depth, height, wd = F.shape
    classes = p_ref.shape[0]
    small = [
        pltpu.make_async_copy(w_hbm, W, sems.at[depth]),
        pltpu.make_async_copy(b_hbm, B, sems.at[depth + 1]),
    ]
    edges = [
        pltpu.make_async_copy(l_hbm.at[:, 0:LHALO], L.at[0], sems.at[depth + 2]),
        pltpu.make_async_copy(l_hbm.at[:, depth - LHALO : depth], L.at[1], sems.at[depth + 3]),
    ]
    planes = [
        pltpu.make_async_copy(f_hbm.at[:, d], F.at[:, d], sems.at[d]) for d in range(depth)
    ]
    for copy in small + planes + edges:
        copy.start()
    for copy in small:
        copy.wait()
    weight = W[...].astype(jnp.float32)
    for k in range(classes):
        for c in range(channels):
            spread_ref[k, c : c + 1, :] = jnp.broadcast_to(weight[k : k + 1, c : c + 1], (1, wd))
    bias = [jnp.broadcast_to(B[0:1, k : k + 1], (height, wd)) for k in range(classes)]
    for d in range(depth):
        planes[d].wait()
        acc = [None] * classes
        for c in range(channels):
            f = F[c, d].astype(jnp.float32)
            for k in range(classes):
                term = jnp.broadcast_to(spread_ref[k, c : c + 1, :], (height, wd)) * f
                acc[k] = term if c == 0 else acc[k] + term
        for k in range(classes):
            prob = 1.0 / (1.0 + jnp.exp(-(acc[k] + bias[k])))
            p_ref[k, d] = prob
            e = jnp.exp(prob * (-1.0 / TAU))
            e_ref[k, d] = e
            if d < HALO:
                first_ref[k, d * height : (d + 1) * height, :] = e
            if d >= depth - HALO:
                at = (d - (depth - HALO)) * height
                last_ref[k, at : at + height, :] = e
    for copy, n, out in zip(edges, range(2), (first_ref, last_ref)):
        copy.wait()
        for k in range(classes):
            for p in range(LHALO):
                at = (HALO + p) * height
                out[k, at : at + height, :] = L[n, k, p].astype(jnp.float32)


VMEM = pl.BlockSpec(memory_space=pltpu.VMEM)
HBM = pl.BlockSpec(memory_space=pltpu.HBM)


def run_head(weight, bias, features, labels):
    classes, channels = weight.shape
    depth, height, wd = features.shape[1:]
    full = jax.ShapeDtypeStruct((classes, depth, height, wd), jnp.float32)
    edge = jax.ShapeDtypeStruct((classes, (HALO + LHALO) * height, wd), jnp.float32)
    return pl.pallas_call(
        head_kernel,
        in_specs=[HBM] * 4,
        out_specs=[VMEM] * 5,
        out_shape=[full, full, edge, edge, jax.ShapeDtypeStruct((classes, channels, wd), jnp.float32)],
        scratch_shapes=[
            pltpu.VMEM(features.shape, features.dtype),
            pltpu.VMEM((2, classes, LHALO, height, wd), jnp.int32),
            pltpu.VMEM(weight.shape, weight.dtype),
            pltpu.VMEM((1, classes), jnp.float32),
            pltpu.SemaphoreType.DMA((depth + 4,)),
        ],
        compiler_params=pltpu.CompilerParams(vmem_limit_bytes=62 * 2**20),
        name="head",
    )(weight, bias.reshape(1, classes), features, labels)


def side_kernel(own_ref, lab_ref, lo_ref, hi_ref, first_ref, last_ref):
    classes, depth, height = own_ref.shape[:3]
    for k in range(classes):
        for out, near in ((first_ref, True), (last_ref, False)):
            base, skip = 0, 0
            for ref, width in ((own_ref, HALO), (lab_ref, LHALO)):
                at = 0 if near else height - width
                for p in range(depth + 2 * width):
                    if p < width:
                        v = lo_ref[k, pl.ds((skip + p) * height + at, width), :]
                    elif p < width + depth:
                        v = ref[k, p - width, pl.ds(at, width), :].astype(jnp.float32)
                    else:
                        v = hi_ref[k, pl.ds((skip + p - width - depth) * height + at, width), :]
                    out[k, pl.ds(base + p * width, width), :] = v
                base += width * (depth + 2 * width)
                skip += width


def run_side(own, labels, lo, hi):
    classes, depth, height, wd = own.shape
    rows = HALO * (depth + 2 * HALO) + LHALO * (depth + 2 * LHALO)
    edge = jax.ShapeDtypeStruct((classes, rows, wd), jnp.float32)
    return pl.pallas_call(
        side_kernel,
        in_specs=[VMEM] * 4,
        out_specs=[VMEM] * 2,
        out_shape=[edge, edge],
        compiler_params=pltpu.CompilerParams(vmem_limit_bytes=16 * 2**20),
        name="side",
    )(own, labels, lo, hi)


def stash(S, group, plane, value):
    height, wd = value.shape
    high = value.astype(jnp.bfloat16)
    low = (value - high.astype(jnp.float32)).astype(jnp.bfloat16)
    for t in range(height // 16):
        at = (plane * (height // 16) + t) * wd
        S[32 * group : 32 * group + 16, at : at + wd] = high[16 * t : 16 * t + 16]
        S[32 * group + 16 : 32 * group + 32, at : at + wd] = low[16 * t : 16 * t + 16]


def contract(f_ref, S):
    channels, depth, height, wd = f_ref.shape
    cols = S.shape[0]
    total = None
    for d in range(0, depth, CHUNK):
        f = jnp.concatenate(
            [
                f_ref[:, d + i, 16 * t : 16 * t + 16, :].reshape(channels * 16, wd)
                for i in range(CHUNK)
                for t in range(height // 16)
            ],
            axis=1,
        )
        n = height // 16 * wd
        got = lax.dot_general(f, S[:, d * n : (d + CHUNK) * n], LAST, preferred_element_type=jnp.float32)
        total = got if total is None else total + got
    h = lax.broadcasted_iota(jnp.int32, (channels, 16, cols), 1)
    g = lax.broadcasted_iota(jnp.int32, (channels, 16, cols), 2) % 16
    return jnp.sum(jnp.where(h == g, total.reshape(channels, 16, cols), 0.0), axis=1)


def collect(m, fields):
    cols = m.shape[1]
    item = lax.broadcasted_iota(jnp.int32, (8, cols), 0)
    at = lax.broadcasted_iota(jnp.int32, (8, cols), 1) // 32
    pick = jnp.zeros((8, cols), jnp.float32)
    for row, group in enumerate(fields):
        if group is not None:
            pick = jnp.where((item == row) & (at == group), 1.0, pick)
    return lax.dot_general(pick, m, LAST, precision=EXACT)


def by_rows(values, lane):
    wd = next(v for v in values if v is not None).shape[1]
    values = [jnp.zeros((1, wd), jnp.float32) if v is None else jnp.sum(v, axis=0, keepdims=True) for v in values]
    values += [jnp.zeros((1, wd), jnp.float32)] * (8 - len(values))
    col = lax.broadcasted_iota(jnp.int32, (wd, wd // 4), 1)
    return jnp.dot(jnp.concatenate(values, axis=0), jnp.where(col == lane, 1.0, 0.0), precision=EXACT)


def early_kernel(f_ref, l_ref, p_ref, k_ref, sum_ref, S):
    classes, depth, height, wd = p_ref.shape
    parts = None
    for k in range(classes):
        sums = [None] * 8
        for d in range(depth):
            prob = p_ref[k, d]
            lab = l_ref[k, d].astype(jnp.float32)
            lsk = k_ref[k, d].astype(jnp.float32)
            slope = prob * (1.0 - prob)
            fields = [slope * lab, slope, slope * lsk]
            for n, v in enumerate([prob * lab, prob, lab, lsk * prob, lsk] + fields):
                sums[n] = v if sums[n] is None else sums[n] + v
            for f, v in enumerate(fields):
                stash(S, k * EARLY + f, d, v)
        here = by_rows(sums[:3] + [None, None] + sums[3:5], k) + by_rows(sums[5:], classes + k)
        parts = here if parts is None else parts + here
    m = contract(f_ref, S)
    heads = [collect(m, [k * EARLY + f for f in range(EARLY)]) for k in range(classes)]
    sum_ref[...] = jnp.concatenate(heads + [parts], axis=1)


def run_early(features, labels, prob, lsk):
    classes, depth, height, wd = prob.shape
    return pl.pallas_call(
        early_kernel,
        in_specs=[VMEM] * 4,
        out_specs=VMEM,
        out_shape=jax.ShapeDtypeStruct((8, wd), jnp.float32),
        scratch_shapes=[pltpu.VMEM((classes * EARLY * 32, depth * (height // 16) * wd), jnp.bfloat16)],
        compiler_params=pltpu.CompilerParams(vmem_limit_bytes=24 * 2**20),
        cost_estimate=pl.CostEstimate(flops=10**9, bytes_accessed=10**7, transcendentals=0),
        name="early",
    )(features, labels, prob, lsk)


def wide_sums(values, lane, band):
    rows, width = values[0].shape
    out = []
    if MXU:
        s = jnp.concatenate(values[:MXU], axis=0)
        high = s.astype(jnp.bfloat16)
        low = (s - high.astype(jnp.float32)).astype(jnp.bfloat16)
        s = jnp.dot(jnp.concatenate([high, low], axis=1), band, preferred_element_type=jnp.float32)
        out = [s[i * rows : (i + 1) * rows] for i in range(MXU)]
    for s in values[MXU:]:
        left = jnp.where(lane == 0, 0.0, pltpu.roll(s, 1, 1))
        right = jnp.where(lane == width - 1, 0.0, pltpu.roll(s, width - 1, 1))
        out.append(s + left + right)
    return out


def boxes(load, d, r0, nr, lane, band):
    h = []
    for i in range(NB + 2):
        h.append(load(d + i - 1, r0 - 1, nr) + load(d + i - 1, r0, nr) + load(d + i - 1, r0 + 1, nr))
    out = []
    for i in range(0, NB, 2):
        mid = h[i + 1] + h[i + 2]
        out.append(h[i] + mid)
        out.append(mid + h[i + 3])
    return wide_sums(out, lane, band)


def sweep(first, last, body):
    for i in range(first, last, NB):
        body(min(i, last - NB))


def core_kernel(
    k, classes,
    before_ref, f_ref, e_own, lo, hi, left, right, l_own, p_own, k_own,
    x_ref, sum_ref,
    E, R, X, U, V, Q, L, S,
):
    depth, height, wd = p_own.shape[1:]
    planes = depth + 2 * HALO
    lplanes = depth + 2 * LHALO
    base = HALO - LHALO

    row = lax.broadcasted_iota(jnp.int32, (2 * wd, wd), 0)
    col = lax.broadcasted_iota(jnp.int32, (2 * wd, wd), 1)
    near = jnp.abs(jnp.where(row < wd, row, row - wd) - col) <= 1
    band = jnp.where(near, 1.0, 0.0).astype(jnp.bfloat16)

    E[0, :, OFF - HALO - 8 : OFF - HALO, :] = jnp.zeros((planes, 8, wd), jnp.float32)
    E[0, :, OFF + height + HALO : OFF + height + HALO + 8, :] = jnp.zeros((planes, 8, wd), jnp.float32)
    L[:, OFF - 8 : OFF - LHALO, :] = jnp.zeros((lplanes, 8 - LHALO, wd), jnp.float32)
    L[:, OFF + height + LHALO : OFF + height + 8, :] = jnp.zeros((lplanes, 8 - LHALO, wd), jnp.float32)

    def gather(put, width, own, skip, base):
        put(slice(width, width + depth), slice(OFF, OFF + height), own[k])
        for p in range(width):
            rows = slice((skip + p) * height, (skip + p + 1) * height)
            put(p, slice(OFF, OFF + height), lo[k, rows, :])
            put(width + depth + p, slice(OFF, OFF + height), hi[k, rows, :])
        for p in range(depth + 2 * width):
            rows = slice(base + p * width, base + (p + 1) * width)
            put(p, slice(OFF - width, OFF), left[k, rows, :])
            put(p, slice(OFF + height, OFF + height + width), right[k, rows, :])

    def put_e(p, rows, v):
        E[0, p, rows, :] = v

    def put_l(p, rows, v):
        L[p, rows, :] = v.astype(jnp.float32)

    gather(put_e, HALO, e_own, 0, 0)
    gather(put_l, LHALO, l_own, HALO, HALO * planes)
    w0, wn = OFF - 8, height + 16
    lane = lax.broadcasted_iota(jnp.int32, (wn, wd), 1)
    lane_big = lax.broadcasted_iota(jnp.int32, (wn + 16, wd), 1)
    lane_own = lax.broadcasted_iota(jnp.int32, (height, wd), 1)

    for j in range(ITERS + 1):
        r0, nr, ln = (w0 - 8, wn + 16, lane_big) if j == 0 else (w0, wn, lane)

        def erode(d, j=j, r0=r0, nr=nr, ln=ln):
            outs = boxes(lambda a, b, n: E[j, a, pl.ds(b, n), :], d, r0, nr, ln, band)
            for i, s in enumerate(outs):
                live = E[0, d + i, pl.ds(r0, nr), :] > 0.0
                E[j + 1, d + i, pl.ds(r0, nr), :] = jnp.where(live, s, 0.0)
                R[j, d + i, pl.ds(r0, nr), :] = jnp.where(live, 1.0 / s, 0.0)

        sweep(j + 1, planes - j - 1, erode)

    for j in range(ITERS + 1):

        def dilate(d, j=j):
            outs = boxes(lambda a, b, n: R[j, a, pl.ds(b, n), :], d, w0, wn, lane, band)
            for i, s in enumerate(outs):
                live = E[0, d + i, pl.ds(w0, wn), :] > 0.0
                rd = 1.0 / s
                t = rd * R[j - 1, d + i, pl.ds(w0, wn), :] if j else rd / E[0, d + i, pl.ds(w0, wn), :]
                U[j, d + i - base, pl.ds(w0, wn), :] = jnp.where(live, rd, 0.0)
                X[j, d + i - base, pl.ds(w0, wn), :] = jnp.where(live, t * t, 0.0)

        sweep(base, planes - base, dilate)

    row = lax.broadcasted_iota(jnp.int32, (wn, wd), 0)
    inner = jnp.where((row >= OFF - w0) & (row < OFF - w0 + height), 1.0, 0.0)

    def point(d, carry):
        rows = pl.ds(w0, wn)
        x = [X[j, d, rows, :] for j in range(ITERS + 1)]
        opx = [1.0 + v for v in x]
        logs = [jnp.log(v) for v in opx]
        skel = SHARP * logs[0]
        om, e, ope = [None], [None], [None]
        for j in range(1, ITERS + 1):
            om.append(1.0 - skel)
            e.append(jnp.exp(logs[j] * om[j]))
            ope.append(1.0 + e[j])
            skel = skel + SHARP * jnp.log(ope[j])
        lab = L[d, rows, :]
        g = None
        for j in range(ITERS, -1, -1):
            if j:
                both = 1.0 / (opx[j] * ope[j])
                gv = x[j] * e[j] * om[j] * both
                keep = 1.0 - (SHARP * logs[j]) * (e[j] * opx[j] * both)
            else:
                gv = x[0] / opx[0]
            if g is not None:
                gv = gv * g
            if j:
                g = keep if g is None else g * keep
            u = gv * U[j, d, rows, :]
            X[j, d, rows, :] = gv
            U[j, d, rows, :] = u
            V[j, d, rows, :] = u * lab
        own = jnp.where((d >= LHALO) & (d < LHALO + depth), 1.0, 0.0)
        skel = skel * (inner * own)
        return carry[0] + skel * lab, carry[1] + skel

    zero = jnp.zeros((wn, wd), jnp.float32)
    sky, sk = lax.fori_loop(0, lplanes, point, (zero, zero), unroll=2)

    for j in range(ITERS + 1, 0, -1):
        now, nxt = j % 2, (j + 1) % 2

        def back(d, j=j, now=now, nxt=nxt):
            b = d - base
            for which, src in ((0, V), (1, U)):
                du = boxes(lambda a, c, n: src[j - 1, a, pl.ds(c, n), :], b, w0, wn, lane, band)
                if j <= ITERS:
                    dq = boxes(lambda a, c, n: Q[which, nxt, a, pl.ds(c, n), :], b, w0, wn, lane, band)
                for i in range(NB):
                    r = R[j - 1, d + i, pl.ds(w0, wn), :]
                    v = -r * du[i]
                    if j <= ITERS:
                        live = E[0, d + i, pl.ds(w0, wn), :] > 0.0
                        gv = X[j, b + i, pl.ds(w0, wn), :]
                        if which == 0:
                            gv = gv * L[b + i, pl.ds(w0, wn), :]
                        v = jnp.where(live, r * (gv + v) + dq[i], 0.0)
                    else:
                        v = r * v
                    Q[which, now, b + i, pl.ds(w0, wn), :] = v

        sweep(HALO - j, planes - HALO + j, back)

    sums = [jnp.zeros((height, wd), jnp.float32) for _ in range(FIELDS - EARLY)]

    def last(d):
        b = d - base
        o = d - HALO
        grads = [
            boxes(lambda a, c, n: Q[which, 1, a, pl.ds(c, n), :], b, OFF, height, lane_own, band)
            for which in range(2)
        ]
        for i in range(NB):
            e = E[0, d + i, pl.ds(OFF, height), :]
            gv = X[0, b + i, pl.ds(OFF, height), :]
            prob = p_own[k, o + i]
            lab = L[b + i, pl.ds(OFF, height), :]
            slope = prob * (1.0 - prob)
            fields = [slope * (gv * lab + e * grads[0][i]), slope * (gv + e * grads[1][i])]
            for f, v in enumerate(fields):
                sums[f] = sums[f] + v
                x_ref[2 + f, o + i] = v
                stash(S, f, o + i, v)
            x_ref[0, o + i] = slope
            x_ref[1, o + i] = lab + 2.0 * k_own[k, o + i].astype(jnp.float32)

    sweep(HALO, HALO + depth, last)
    parts = by_rows([None] * 3 + [sky, sk], k) + by_rows([None] * EARLY + sums, classes + k)
    heads = collect(contract(f_ref, S), [None] * EARLY + [0, 1])
    blank = jnp.zeros_like(heads)
    whole = jnp.concatenate([heads if n == k else blank for n in range(classes)] + [parts], axis=1)
    whole = whole + before_ref[...]
    for n in range(sum_ref.shape[0]):
        sum_ref[n] = whole


def run_core(k, copies, before, features, own, near, labels, prob, lsk):
    classes, depth, height, wd = prob.shape
    planes = depth + 2 * HALO
    lplanes = depth + 2 * LHALO
    args = (before, features, own, *near, labels, prob, lsk)
    n = ITERS + 1
    fields = jax.ShapeDtypeStruct((4, depth, height, wd), jnp.float32)
    sums = jax.ShapeDtypeStruct((copies, 8, wd), jnp.float32)
    return pl.pallas_call(
        functools.partial(core_kernel, k, classes),
        in_specs=[VMEM] * len(args),
        out_specs=[VMEM] * 2,
        out_shape=[fields, sums],
        scratch_shapes=[
            pltpu.VMEM((n + 1, planes, ROWS, wd), jnp.float32),
            pltpu.VMEM((n, planes, ROWS, wd), jnp.float32),
            pltpu.VMEM((n, lplanes, ROWS, wd), jnp.float32),
            pltpu.VMEM((n, lplanes, ROWS, wd), jnp.float32),
            pltpu.VMEM((n, lplanes, ROWS, wd), jnp.float32),
            pltpu.VMEM((2, 2, lplanes, ROWS, wd), jnp.float32),
            pltpu.VMEM((lplanes, ROWS, wd), jnp.float32),
            pltpu.VMEM(((FIELDS - EARLY) * 32, depth * (height // 16) * wd), jnp.bfloat16),
        ],
        compiler_params=pltpu.CompilerParams(vmem_limit_bytes=34 * 2**20),
        cost_estimate=pl.CostEstimate(flops=2 * 10**10, bytes_accessed=4 * 10**7, transcendentals=0),
        name=f"core{k}",
    )(*args)


def middle_kernel(in_ref, out_ref):
    total = jnp.sum(in_ref[...], axis=0)
    for n in range(out_ref.shape[0]):
        out_ref[n] = total


def run_middle(copies, parts):
    return pl.pallas_call(
        middle_kernel,
        in_specs=[VMEM],
        out_specs=VMEM,
        out_shape=jax.ShapeDtypeStruct((copies,) + parts.shape[1:], jnp.float32),
        compiler_params=pltpu.CompilerParams(vmem_limit_bytes=2 * 2**20),
        name="middle",
    )(parts)


def tail_kernel(cells, w_ref, s_ref, *refs):
    classes = len(refs) - 5
    x_ref = refs[:classes]
    g_ref, loss_ref, gw_ref, gb_ref, C = refs[classes:]
    channels = g_ref.shape[0]
    quarter = s_ref.shape[2] // 4
    wd = s_ref.shape[2]

    @pl.when(pl.program_id(0) == 0)
    def _():
        total = jnp.sum(s_ref[...], axis=0)
        tp, sp, sl, sky, sk, lsp, ls = [jnp.broadcast_to(total[i : i + 1], total.shape) for i in range(7)]
        prec = (sky + 1.0) / (sk + 1.0)
        sens = (lsp + 1.0) / (ls + 1.0)
        both = prec + sens
        cldice = 1.0 - 2.0 * prec * sens / both
        bottom = tp + ALPHA * (sp - tp) + BETA * (sl - tp) + 1.0
        tversky = (tp + 1.0) / bottom
        term = cldice + 1.0 - tversky
        scale = cells / classes
        by_prec = -2.0 * (sens / both) * (sens / both) * scale
        by_sens = -2.0 * (prec / both) * (prec / both) * scale
        by_sky = by_prec / (sk + 1.0)
        by_sk = -by_sky * prec
        by_lsp = by_sens / (ls + 1.0)
        by_sp = scale * ALPHA * tversky / bottom
        by_tp = scale * (tversky * (1.0 - ALPHA - BETA) - 1.0) / bottom
        lane = lax.broadcasted_iota(jnp.int32, total.shape, 1)
        item = lax.broadcasted_iota(jnp.int32, total.shape, 0)
        mult = jnp.zeros_like(total)
        loss = jnp.zeros_like(total)
        for k in range(classes):
            mine = (lane // quarter == k) | (lane == classes * (quarter + 1) + k)
            spot = lane == classes * quarter + k

            def pick(v):
                return jnp.sum(jnp.where(spot, v, 0.0), axis=1, keepdims=True)

            for f, v in enumerate((by_tp, by_sp, by_lsp, by_sky, by_sk)):
                v = jnp.broadcast_to(pick(v), total.shape)
                C[k, f] = v
                mult = jnp.where(mine & (item == f), v, mult)
            loss = loss + pick(term) * (1.0 / classes)
        grad = jnp.sum(jnp.where(item < FIELDS, total * mult, 0.0), axis=0, keepdims=True)
        square = jnp.sum(grad * grad, axis=1, keepdims=True)
        rms = jnp.sqrt(square / (classes * channels + classes) + 1e-06)
        grad = grad / rms
        loss_ref[...] = loss[0:1, 0:1]
        gw_ref[...] = jnp.concatenate([grad[:, k * quarter : (k + 1) * quarter] for k in range(classes)], axis=0)
        n = classes * (quarter + 1)
        gb_ref[...] = grad[:, n : n + classes]

    height = g_ref.shape[2]
    base = pl.program_id(0) * g_ref.shape[1]
    for p in range(g_ref.shape[1]):
        for t in range(height // 16):
            rows = slice(16 * t, 16 * t + 16)
            dlogit = []
            for k in range(classes):
                c = [jnp.concatenate([C[k, f]] * 2, axis=0) for f in range(FIELDS)]
                slope, code, ga, gb = [x_ref[k][f, base + p, rows, :] for f in range(4)]
                lsk = code >= 2.0
                lab = jnp.where(lsk, code - 2.0, code)
                v = slope * (c[0] * lab + c[1] + jnp.where(lsk, c[2], 0.0)) + c[3] * ga + c[4] * gb
                dlogit.append(v)
            for c in range(channels):
                v = None
                for k in range(classes):
                    term = jnp.broadcast_to(w_ref[k, c : c + 1, :], (16, wd)) * dlogit[k]
                    v = term if v is None else v + term
                g_ref[c, p, rows, :] = v.astype(jnp.bfloat16)


def run_tail(cells, spread, sums, fields):
    depth, height, wd = fields[0].shape[1:]
    classes, channels = spread.shape[:2]
    step = 2
    return pl.pallas_call(
        functools.partial(tail_kernel, cells),
        grid=(depth // step,),
        in_specs=[VMEM] * (2 + classes),
        out_specs=[
            pl.BlockSpec((channels, step, height, wd), lambda d: (0, d, 0, 0)),
            pl.BlockSpec((1, 1), lambda d: (0, 0)),
            pl.BlockSpec((classes, channels), lambda d: (0, 0)),
            pl.BlockSpec((1, classes), lambda d: (0, 0)),
        ],
        out_shape=[
            jax.ShapeDtypeStruct((channels, depth, height, wd), jnp.bfloat16),
            jax.ShapeDtypeStruct((1, 1), jnp.float32),
            jax.ShapeDtypeStruct((classes, channels), jnp.float32),
            jax.ShapeDtypeStruct((1, classes), jnp.float32),
        ],
        scratch_shapes=[pltpu.VMEM((classes, FIELDS, 8, wd), jnp.float32)],
        compiler_params=pltpu.CompilerParams(vmem_limit_bytes=16 * 2**20),
        name="tail",
    )(spread, sums, *fields)


def per_device(features, head_weight, head_bias, labels, label_skeleton):
    classes, channels = head_weight.shape
    _, block_d, block_h, wd = features.shape
    cells = block_d * lax.axis_size("depth") * block_h * lax.axis_size("height") * wd
    prob, own, first, last, spread = run_head(head_weight, head_bias, features, labels)
    lo, hi = shift(last, "depth", 1), shift(first, "depth", -1)
    local = run_early(features, labels, prob, label_skeleton)
    lo, hi, local = lax.optimization_barrier((lo, hi, local))
    first, last = run_side(own, labels, lo, hi)
    near = (lo, hi, shift(last, "height", 1), shift(first, "height", -1))
    fields = []
    for k in range(classes):
        copies = lax.axis_size("height") if k == classes - 1 else 1
        mine, local = run_core(k, copies, local, features, own, near, labels, prob, label_skeleton)
        fields.append(mine)
        if copies == 1:
            local = local[0]
    part = run_middle(lax.axis_size("depth"), lax.all_to_all(local, "height", 0, 0, tiled=True))
    parts = lax.all_to_all(part, "depth", 0, 0, tiled=True)
    grad_features, loss, grad_w, grad_b = run_tail(cells, spread, parts, fields)
    return loss[0, 0], grad_features, grad_w, grad_b[0]


def solution(mesh):
    return jax.shard_map(
        per_device,
        mesh=mesh,
        in_specs=(
            P(None, "depth", "height", None),
            P(),
            P(),
            P(None, "depth", "height", None),
            P(None, "depth", "height", None),
        ),
        out_specs=(P(), P(None, "depth", "height", None), P(), P()),
        check_vma=False,
    )
```
